32 devices in a mesh: brick: 16 (over z, x, core), pme: 2 (over y).
Axes of the slice: x: 2, y: 2, z: 4, core: 2. Of those that a mesh axis runs over, the one named last changes fastest.
Arguments:
- features: bfloat16 [4096, 512], P(('brick', 'pme')), may hold values from -6 to 6
- cotangent: bfloat16 [4096, 1152], P(('brick', 'pme')), may hold values from -6 to 6
- neighbor_index: int32 [262144], P(('brick', 'pme')), may hold values from 0 to 319
- neighbor_count: int32 [4096], P(('brick', 'pme')), may hold values from 1 to 64, as said below
- edge_vector: float32 [3, 262144], P(None, ('brick', 'pme')), may hold values from -2.7 to 2.7, as said below
- quad_index: int32 [32, 2, 2, 16], P(('brick', 'pme')), may hold values from 0 to 127, as said below
- weight_basis: float32 [8, 64], replicated, may hold values from -2 to 2
- weight_radial: bfloat16 [64, 896], replicated, may hold values from -0.75 to 0.75
- weight_scalar: float32 [128, 128], replicated, may hold values from -0.5 to 0.5
- weight_gate: float32 [128, 256], replicated, may hold values from -0.5 to 0.5
- weight_vector: float32 [128, 128], replicated, may hold values from -0.5 to 0.5
- weight_tensor: float32 [128, 128], replicated, may hold values from -0.5 to 0.5
- weight_charge: float32 [128], replicated, may hold values from -0.5 to 0.5
- grid_base: int32 [3, 4096], P(None, ('brick', 'pme')), may hold values from 0 to 191, as said below
- grid_frac: float32 [3, 4096], P(None, ('brick', 'pme')), may hold values from -0.5 to 0.5
Outputs:
- updated: bfloat16 [4096, 1152], P(('brick', 'pme'))
- feature_grad: float32 [4096, 512], P(('brick', 'pme'))
- potential: float32 [96, 48, 192], P('brick', 'pme')
The draws below stay inside these ranges and needn't reach their ends.
Inputs may be any that keep to these rules, and one draw needn't show every extreme that they name: `neighbor_index`: values below 128 name the device's own rows; 128 + m * 16 + g names row g of the m-th border block. `neighbor_count`: slots below the count are live, the rest padding; counts cluster by device. `edge_vector`: every component has magnitude between 0.5 and 2.7. `quad_index`: the 64 entries of one device are distinct. `grid_base`: row 0 is below 6, row 1 below 24, row 2 below 192.
All inputs are finite; a program needn't handle non-finite values.
Results may differ from the reference program's by a relative error of at most 0.004.
Values may be sent and summed in bfloat16 or wider, within the bound.
No kernel may reach another device: no remote copies, remote signals or barrier semaphores. Data moves between devices by JAX's collectives and lax.ppermute only.
A program may use at most 128 MiB of HBM per device.

```python
import math
import jax
import jax.numpy as jnp
import numpy as np
from jax import lax

C = 128
NB = 8
RH = 64
NBR = 64
ATOM_DEV = 128
GHOST = 16
GX = 6
GY = 24
NGZ = 192
NGX = 96
NGY = 48
ATOMS = 4096
N_BRICK = 16
N_PME = 2
DEVICES = 32


def draw_neighbor_count(key, part):
    key = jax.random.fold_in(key, 11)
    level_key, jitter_key = jax.random.split(key)
    devices_all = ATOMS // ATOM_DEV
    level = jax.random.randint(level_key, (devices_all, 1), NBR // 4, NBR + 1)
    jitter = jax.random.randint(jitter_key, (devices_all, ATOM_DEV), -(NBR // 8), NBR // 8 + 1)
    counts = jnp.clip(level + jitter, 1, NBR).reshape(ATOMS)
    return counts.at[0].set(NBR).astype(jnp.int32)


def draw_edge_vector(key, part):
    key = jax.random.fold_in(key, 12)
    sign_key, size_key = jax.random.split(key)
    signs = jnp.where(jax.random.bernoulli(sign_key, 0.5, (3, ATOMS * NBR)), 1.0, -1.0)
    magnitude = jax.random.uniform(size_key, (3, ATOMS * NBR), jnp.float32, 0.5, 2.7)
    return (signs * magnitude).astype(jnp.float32)


def draw_quad_index(key, part):
    key = jax.random.fold_in(key, 13)
    device_keys = jax.random.split(key, DEVICES)

    def pick_rows(single_key):
        return jax.random.permutation(single_key, ATOM_DEV)[:4 * GHOST]
    chosen = jax.vmap(pick_rows)(device_keys)
    return chosen.reshape(DEVICES, 2, 2, GHOST).astype(jnp.int32)


def draw_grid_base(key, part):
    key = jax.random.fold_in(key, 14)
    key_x, key_y, key_z = jax.random.split(key, 3)
    along_x = jax.random.randint(key_x, (1, ATOMS), 0, GX)
    along_y = jax.random.randint(key_y, (1, ATOMS), 0, GY)
    along_z = jax.random.randint(key_z, (1, ATOMS), 0, NGZ)
    return jnp.concatenate([along_x, along_y, along_z], axis=0).astype(jnp.int32)


def set_ends(values, rng, low, top_value):
    place = [jax.random.randint(jax.random.fold_in(rng, axis), (), 0, length) for axis, length in enumerate(values.shape)]
    longest = values.shape.index(max(values.shape))
    next_to = place[:longest] + [(place[longest] + 1) % values.shape[longest]] + place[longest + 1:]
    return values.at[tuple(place)].set(low).at[tuple(next_to)].set(top_value)


def level_of(key, extent, shards, low, high):
    factor_of, own = 1.0, jax.random.fold_in(key, 6)
    for position, shards_of in shards:
        heights = jnp.exp(jax.random.uniform(jax.random.fold_in(own, position), (shards_of,), jnp.float32, low / len(shards), high / len(shards)))
        factor_of = factor_of * jnp.repeat(heights, extent[position] // shards_of).reshape([-1 if axis == position else 1 for axis in range(len(extent))])
    return factor_of


def gaussian(own_key, dims, width, reach, shards=(), held_as=jnp.bfloat16):
    values = jax.random.normal(own_key, dims, jnp.float32) * width
    if len(shards) > 0:
        values = level_of(own_key, dims, shards, -0.22, 0.18) * values
    return jnp.clip(values, min=-reach, max=reach).astype(held_as)


def setup_inputs(seed: int = 0) -> dict:
    splits = jax.random.split(jax.random.key(seed), 16)
    features = gaussian(splits[0], (ATOMS, 4 * C), 1.0, 6.0, ((0, 32),))
    cotangent = gaussian(splits[1], (ATOMS, 9 * C), 1.0, 6.0, ((0, 32),))
    neighbor_index = set_ends(jax.random.randint(splits[2], (ATOMS * NBR,), 0, ATOM_DEV + 12 * GHOST), jax.random.fold_in(splits[2], 1), 0, (ATOM_DEV + 12 * GHOST) - 1).astype(jnp.int32)
    neighbor_count = draw_neighbor_count(jax.random.fold_in(splits[15], 71), 0)
    edge_vector = draw_edge_vector(jax.random.fold_in(splits[15], 71), 0)
    quad_index = draw_quad_index(jax.random.fold_in(splits[15], 71), 0)
    weight_basis = gaussian(splits[6], (NB, RH), NB ** -0.5, 2.0, (), jnp.float32)
    weight_radial = gaussian(splits[7], (RH, 7 * C), RH ** -0.5, 0.75)
    weight_scalar = gaussian(splits[8], (C, C), C ** -0.5, 0.5, (), jnp.float32)
    weight_gate = gaussian(splits[9], (C, 2 * C), C ** -0.5, 0.5, (), jnp.float32)
    weight_vector = gaussian(splits[10], (C, C), C ** -0.5, 0.5, (), jnp.float32)
    weight_tensor = gaussian(splits[11], (C, C), C ** -0.5, 0.5, (), jnp.float32)
    weight_charge = gaussian(splits[12], (C,), C ** -0.5, 0.5, (), jnp.float32)
    grid_base = draw_grid_base(jax.random.fold_in(splits[15], 71), 0)
    grid_frac = jnp.clip(jax.random.uniform(splits[14], (3, ATOMS), jnp.float32, -0.5, 0.5) * level_of(splits[14], (3, ATOMS), ((1, 32),), -0.4, 0.0), -0.5, 0.5)
    return {"features": features, "cotangent": cotangent, "neighbor_index": neighbor_index, "neighbor_count": neighbor_count, "edge_vector": edge_vector, "quad_index": quad_index, "weight_basis": weight_basis, "weight_radial": weight_radial, "weight_scalar": weight_scalar, "weight_gate": weight_gate, "weight_vector": weight_vector, "weight_tensor": weight_tensor, "weight_charge": weight_charge, "grid_base": grid_base, "grid_frac": grid_frac}


CUTOFF = 5.0
SMEAR = 1.0
COUPLING = 0.1
PRECISE = lax.Precision.HIGHEST
BORDER = ((0, 0), (0, 1), (0, 2), (0, 3), (1, 0), (1, 3), (2, 0), (2, 3), (3, 0), (3, 1), (3, 2), (3, 3))

def side_tables():
    shift_table = {0: -1, 1: 0, 2: 0, 3: 1}
    quarter_table = {0: 1, 1: 0, 2: 1, 3: 0}
    shift_rows = np.array([shift_table[border_cell[0]] for border_cell in BORDER], dtype=np.int32)
    quarter_rows = np.array([quarter_table[border_cell[0]] for border_cell in BORDER], dtype=np.int32)
    shift_cols = np.array([shift_table[border_cell[1]] for border_cell in BORDER], dtype=np.int32)
    quarter_cols = np.array([quarter_table[border_cell[1]] for border_cell in BORDER], dtype=np.int32)
    return (shift_rows, quarter_rows, shift_cols, quarter_cols)

def edge_messages(sender, direction, radial, channels):
    scalar = sender[:, :channels]
    vector = [sender[:, channels * (1 + axis_id):channels * (2 + axis_id)] for axis_id in range(3)]
    unit_cols = [direction[axis_id][:, None] for axis_id in range(3)]
    path_weights = [radial[:, channels * path_id:channels * (path_id + 1)] for path_id in range(7)]
    projection = unit_cols[0] * vector[0] + unit_cols[1] * vector[1] + unit_cols[2] * vector[2]
    pieces = [path_weights[0] * scalar + path_weights[1] * projection]
    for axis_id in range(3):
        pieces.append(path_weights[2] * scalar * unit_cols[axis_id] + path_weights[3] * vector[axis_id] + path_weights[4] * (unit_cols[axis_id] * projection - vector[axis_id] / 3.0))
    for left_axis, right_axis in ((0, 0), (1, 1), (0, 1), (1, 2), (0, 2)):
        shape_term = unit_cols[left_axis] * unit_cols[right_axis]
        mixed_term = 0.5 * (unit_cols[left_axis] * vector[right_axis] + unit_cols[right_axis] * vector[left_axis])
        if left_axis == right_axis:
            shape_term = shape_term - 1.0 / 3.0
            mixed_term = mixed_term - projection / 3.0
        pieces.append(path_weights[5] * scalar * shape_term + path_weights[6] * mixed_term)
    return jnp.concatenate(pieces, axis=1)

def layer_rows(table_rows, slot_index, own_rows, edge_rows, live_count, params):
    weight_basis, weight_radial, weight_scalar, weight_gate, weight_vector, weight_tensor = params
    atom_rows, slot_total = slot_index.shape
    channels = own_rows.shape[1] // 4
    sender = jnp.take(table_rows, slot_index.reshape(-1), axis=0)
    flat_vector = edge_rows.reshape(3, -1)
    distance = jnp.sqrt(flat_vector[0] * flat_vector[0] + flat_vector[1] * flat_vector[1] + flat_vector[2] * flat_vector[2])
    direction = flat_vector / distance[None, :]
    orders = jnp.arange(1, weight_basis.shape[0] + 1, dtype=jnp.int32).astype(jnp.float32)
    envelope = 0.5 * (jnp.cos(jnp.pi * distance / CUTOFF) + 1.0)
    basis_rows = jnp.sin(jnp.pi / CUTOFF * distance[:, None] * orders[None, :]) * envelope[:, None]
    hidden = jax.nn.silu(jnp.dot(basis_rows, weight_basis, precision=PRECISE)).astype(jnp.bfloat16)
    radial = jnp.dot(hidden, weight_radial, preferred_element_type=jnp.float32)
    live_slot = jnp.arange(slot_total, dtype=jnp.int32)[None, :] < live_count[:, None]
    radial = radial * live_slot.reshape(-1, 1).astype(jnp.float32)
    messages = edge_messages(sender, direction, radial, channels)
    aggregate = messages.reshape(atom_rows, slot_total, 9 * channels).sum(axis=1) * (1.0 / math.sqrt(slot_total))
    aggregate_s = aggregate[:, :channels]
    gate_values = jax.nn.sigmoid(jnp.dot(aggregate_s, weight_gate, precision=PRECISE))
    blocks_out = [own_rows[:, :channels] + jax.nn.silu(jnp.dot(aggregate_s, weight_scalar, precision=PRECISE))]
    for axis_id in range(3):
        lower = channels * (1 + axis_id)
        blocks_out.append(own_rows[:, lower:lower + channels] + gate_values[:, :channels] * jnp.dot(aggregate[:, lower:lower + channels], weight_vector, precision=PRECISE))
    for tensor_id in range(5):
        lower = channels * (4 + tensor_id)
        blocks_out.append(gate_values[:, channels:] * jnp.dot(aggregate[:, lower:lower + channels], weight_tensor, precision=PRECISE))
    return jnp.concatenate(blocks_out, axis=1)

def spline_weights(offset):
    return (0.5 * (0.5 - offset) * (0.5 - offset), 0.75 - offset * offset, 0.5 * (0.5 + offset) * (0.5 + offset))

def influence(index_x, index_y, index_z, points_x, points_y, points_z):
    summed = 0.0
    correct = 1.0
    for index_k, points in ((index_x, points_x), (index_y, points_y), (index_z, points_z)):
        folded = jnp.minimum(index_k, points - index_k).astype(jnp.float32) / points
        modulus = 0.75 + 0.25 * jnp.cos(2.0 * jnp.pi / points * index_k.astype(jnp.float32))
        summed = summed + folded * folded
        correct = correct / (modulus * modulus)
    nonzero = summed > 0.0
    safe_sum = jnp.where(nonzero, summed, 1.0)
    value = COUPLING * jnp.exp(-2.0 * jnp.pi * jnp.pi * SMEAR * SMEAR * summed) / safe_sum * correct
    return jnp.where(nonzero, value, 0.0)

def reference(features, cotangent, neighbor_index, neighbor_count, edge_vector, quad_index, weight_basis, weight_radial, weight_scalar, weight_gate, weight_vector, weight_tensor, weight_charge, grid_base, grid_frac):
    neighbor_index = neighbor_index.reshape(ATOMS, NBR)
    edge_vector = edge_vector.reshape(3, ATOMS, NBR)
    shift_rows, quarter_rows, shift_cols, quarter_cols = side_tables()
    shift_rows = jnp.asarray(shift_rows, dtype=jnp.int32)
    quarter_rows = jnp.asarray(quarter_rows, dtype=jnp.int32)
    shift_cols = jnp.asarray(shift_cols, dtype=jnp.int32)
    quarter_cols = jnp.asarray(quarter_cols, dtype=jnp.int32)
    atom_ids = jnp.arange(ATOMS, dtype=jnp.int32)
    device_ids = atom_ids // ATOM_DEV
    brick_ids = device_ids // N_PME
    pme_ids = device_ids % N_PME
    is_ghost = neighbor_index >= ATOM_DEV
    ghost_slot = jnp.maximum(neighbor_index - ATOM_DEV, 0)
    border_id = ghost_slot // GHOST
    ghost_row = ghost_slot % GHOST
    source = (brick_ids[:, None] + shift_rows[border_id]) % N_BRICK * N_PME + (pme_ids[:, None] + shift_cols[border_id]) % N_PME
    remote = source * ATOM_DEV + quad_index[source, quarter_rows[border_id], quarter_cols[border_id], ghost_row]
    sender = jnp.where(is_ghost, remote, device_ids[:, None] * ATOM_DEV + neighbor_index).astype(jnp.int32)
    params = (weight_basis, weight_radial, weight_scalar, weight_gate, weight_vector, weight_tensor)
    block_atoms = 64
    block_total = ATOMS // block_atoms

    def forward(table_rows):

        def one_block(block_id):
            first_row = block_id * block_atoms
            own_rows = lax.dynamic_slice_in_dim(table_rows, first_row, block_atoms, 0)
            slot_index = lax.dynamic_slice_in_dim(sender, first_row, block_atoms, 0)
            edge_rows = lax.dynamic_slice_in_dim(edge_vector, first_row, block_atoms, 1)
            live_count = lax.dynamic_slice_in_dim(neighbor_count, first_row, block_atoms, 0)
            return layer_rows(table_rows, slot_index, own_rows, edge_rows, live_count, params)
        result = lax.map(jax.checkpoint(one_block), jnp.arange(block_total, dtype=jnp.int32))
        return result.reshape(ATOMS, 9 * C)
    updated32, pullback = jax.vjp(forward, features.astype(jnp.float32))
    feature_grad = pullback(cotangent.astype(jnp.float32))[0]
    updated = updated32.astype(jnp.bfloat16)
    charge = jnp.dot(updated[:, :C].astype(jnp.float32), weight_charge, precision=PRECISE)
    global_x = brick_ids * GX + grid_base[0]
    global_y = pme_ids * GY + grid_base[1]
    global_z = grid_base[2]
    weights_x = spline_weights(grid_frac[0])
    weights_y = spline_weights(grid_frac[1])
    weights_z = spline_weights(grid_frac[2])
    charge_grid = jnp.zeros((NGX, NGY, NGZ), jnp.float32)
    for step_x in range(3):
        for step_y in range(3):
            for step_z in range(3):
                charge_grid = charge_grid.at[(global_x + step_x - 1) % NGX, (global_y + step_y - 1) % NGY, (global_z + step_z - 1) % NGZ].add(charge * weights_x[step_x] * weights_y[step_y] * weights_z[step_z])
    index_x = jnp.arange(NGX, dtype=jnp.int32)[:, None, None]
    index_y = jnp.arange(NGY, dtype=jnp.int32)[None, :, None]
    index_z = jnp.arange(NGZ, dtype=jnp.int32)[None, None, :]
    kernel = influence(index_x, index_y, index_z, NGX, NGY, NGZ)
    potential = jnp.real(jnp.fft.ifftn(jnp.fft.fftn(charge_grid) * kernel)).astype(jnp.float32)
    return (updated, feature_grad, potential)
```

```python
import functools
import math

import jax
import jax.numpy as jnp
from jax import lax
from jax.experimental import pallas as pl
from jax.experimental.pallas import tpu as pltpu
from jax.sharding import PartitionSpec as P

GX = 6
GY = 24
NGZ = 192

CUTOFF = 5.0
SMEAR = 1.0
COUPLING = 0.1
PRECISE = lax.Precision.HIGHEST
BORDER = ((0, 0), (0, 1), (0, 2), (0, 3), (1, 0), (1, 3), (2, 0), (2, 3), (3, 0), (3, 1), (3, 2), (3, 3))
SHIFT = (-1, 0, 0, 1)
QUARTER = (1, 0, 1, 0)
SLOT_BLOCK = 8
ROW_GROUP = 16
VMEM_LIMIT = 48 * 1024 * 1024


def halo_groups(brick_count, pme_count):
    groups = {}
    for cell, (row, col) in enumerate(BORDER):
        step = (SHIFT[row] % brick_count, SHIFT[col] % pme_count)
        groups.setdefault(step, []).append(cell)
    return tuple((step, tuple(cells)) for step, cells in groups.items())


def shifted(value, brick_step, pme_step):
    bricks, pmes = lax.axis_size("brick"), lax.axis_size("pme")
    pairs = []
    for b in range(bricks):
        for p in range(pmes):
            source = (b + brick_step) % bricks * pmes + (p + pme_step) % pmes
            pairs.append((source, b * pmes + p))
    return lax.ppermute(value, ("brick", "pme"), pairs)


def dot_t(left, right, dims, precision=None):
    return lax.dot_general(
        left, right, (dims, ((), ())), precision=precision, preferred_element_type=jnp.float32
    )


def dot_f32(left, right, dims=((1,), (0,))):
    return dot_t(left, right, dims, PRECISE)


def params(**kwargs):
    return pltpu.CompilerParams(vmem_limit_bytes=VMEM_LIMIT, **kwargs)


def pack_kernel(groups, quad_ref, features_ref, *message_refs):
    atoms = features_ref.shape[0]
    ghost = quad_ref.shape[3]
    rows = lax.broadcasted_iota(jnp.int32, (atoms, ghost), 0)
    picked = {}
    for row in range(2):
        for col in range(2):
            chosen = (rows == quad_ref[0, row, col : col + 1, :]).astype(jnp.bfloat16)
            picked[row, col] = dot_t(chosen, features_ref[...], ((0,), (0,))).astype(jnp.bfloat16)
    for (_, cells), message_ref in zip(groups, message_refs):
        for place, cell in enumerate(cells):
            row, col = BORDER[cell]
            message_ref[place * ghost : (place + 1) * ghost, :] = picked[QUARTER[row], QUARTER[col]]


def radial_kernel(vector_ref, count_ref, basis_weight_ref, hidden_ref, unit_ref, basis_ref):
    slots, atoms = vector_ref.shape[1:]
    orders = basis_weight_ref.shape[0]
    parts = [vector_ref[axis] for axis in range(3)]
    distance = jnp.sqrt(parts[0] * parts[0] + parts[1] * parts[1] + parts[2] * parts[2])
    inverse = 1.0 / distance
    for axis in range(3):
        unit_ref[axis] = parts[axis] * inverse
    theta = distance * (math.pi / CUTOFF)
    cosine = jnp.cos(theta)
    live = lax.broadcasted_iota(jnp.int32, (slots, atoms), 0) < count_ref[...]
    envelope = jnp.where(live, 0.5 * (cosine + 1.0), 0.0)
    before = jnp.zeros_like(theta)
    current = jnp.sin(theta) * envelope
    for order in range(orders):
        for slot in range(slots):
            basis_ref[order : order + 1, slot * atoms : (slot + 1) * atoms] = current[slot : slot + 1, :]
        before, current = current, 2.0 * cosine * current - before
    width = SLOT_BLOCK * atoms
    for start in range(0, slots * atoms, width):
        inner = dot_f32(basis_weight_ref[...], basis_ref[:, start : start + width], ((0,), (0,)))
        hidden_ref[:, start : start + width] = (inner * jax.nn.sigmoid(inner)).astype(jnp.bfloat16)


def load_radial_weight(weight_ref, weight_t_ref):
    channels = weight_ref.shape[1] // 7
    for path in range(7):
        block = weight_ref[:, path * channels : (path + 1) * channels].astype(jnp.float32)
        if path == 3:
            block = block - weight_ref[:, 4 * channels : 5 * channels].astype(jnp.float32) * (1.0 / 3.0)
        weight_t_ref[path * channels : (path + 1) * channels, :] = block.T.astype(jnp.bfloat16)


def sender_onehot(index_ref, table_rows):
    slots, atoms = index_ref.shape
    rows = lax.broadcasted_iota(jnp.int32, (table_rows, atoms), 0)
    return jnp.concatenate(
        [(rows == index_ref[slot : slot + 1, :]).astype(jnp.bfloat16) for slot in range(slots)], axis=1
    )


def forward_kernel(
    groups,
    hidden_ref,
    unit_ref,
    index_ref,
    features_ref,
    weight_radial_ref,
    weight_scalar_ref,
    weight_gate_ref,
    weight_vector_ref,
    weight_tensor_ref,
    weight_charge_ref,
    cotangent_ref,
    *rest,
):
    message_refs = rest[: len(groups)]
    updated_ref, charge_ref, node_grad_ref = rest[len(groups) : len(groups) + 3]
    table_ref, table_t_ref, weight_t_ref, radial_ref, sender_ref, total_ref = rest[len(groups) + 3 :]
    step = pl.program_id(0)
    atoms, width = features_ref.shape
    channels = width // 4
    ghost = (table_ref.shape[0] - atoms) // 12
    slots = index_ref.shape[0]

    @pl.when(step == 0)
    def _():
        table_ref[:atoms, :] = features_ref[...]
        for (_, cells), message_ref in zip(groups, message_refs):
            for place, cell in enumerate(cells):
                lower = atoms + cell * ghost
                table_ref[lower : lower + ghost, :] = message_ref[place * ghost : (place + 1) * ghost, :]
        for block in range(4):
            piece = table_ref[:, block * channels : (block + 1) * channels].astype(jnp.float32)
            table_t_ref[block * channels : (block + 1) * channels, :] = piece.T.astype(jnp.bfloat16)
        load_radial_weight(weight_radial_ref, weight_t_ref)
        total_ref[...] = jnp.zeros_like(total_ref)

    sender_ref[...] = dot_t(
        table_t_ref[...], sender_onehot(index_ref, table_ref.shape[0]), ((1,), (0,))
    )
    radial_ref[...] = dot_t(weight_t_ref[...], hidden_ref[...], ((1,), (0,)))

    def group(number, carry):
        row = pl.multiple_of(number * ROW_GROUP, ROW_GROUP)
        total = [total_ref[block, pl.ds(row, ROW_GROUP), :] for block in range(10)]
        for slot in range(slots):
            lanes = slice(slot * atoms, (slot + 1) * atoms)
            unit = [unit_ref[axis, slot : slot + 1, :] for axis in range(3)]
            paths = [radial_ref[pl.ds(path * channels + row, ROW_GROUP), lanes] for path in range(7)]
            scalar = sender_ref[pl.ds(row, ROW_GROUP), lanes]
            vector = [
                sender_ref[pl.ds((1 + axis) * channels + row, ROW_GROUP), lanes] for axis in range(3)
            ]
            along = unit[0] * vector[0] + unit[1] * vector[1] + unit[2] * vector[2]
            total[0] = total[0] + (paths[0] * scalar + paths[1] * along)
            pushed = paths[2] * scalar + paths[4] * along
            twisted = paths[5] * scalar
            mixed = []
            for axis in range(3):
                total[1 + axis] = total[1 + axis] + (unit[axis] * pushed + paths[3] * vector[axis])
                mixed.append(unit[axis] * twisted + paths[6] * vector[axis])
                total[4 + axis] = total[4 + axis] + unit[axis] * mixed[axis]
            for place, (left, right) in enumerate(((0, 1), (1, 2), (0, 2))):
                total[7 + place] = total[7 + place] + (
                    unit[left] * mixed[right] + unit[right] * mixed[left]
                )
        for block in range(10):
            total_ref[block, pl.ds(row, ROW_GROUP), :] = total[block]
        return carry

    lax.fori_loop(0, channels // ROW_GROUP, group, 0)

    @pl.when(step == pl.num_programs(0) - 1)
    def _():
        scale = 1.0 / math.sqrt(slots * pl.num_programs(0))
        trace = (total_ref[4] + total_ref[5] + total_ref[6]) * (1.0 / 3.0)
        blocks = [total_ref[0], total_ref[1], total_ref[2], total_ref[3]]
        blocks += [total_ref[4] - trace, total_ref[5] - trace]
        blocks += [0.5 * total_ref[7], 0.5 * total_ref[8], 0.5 * total_ref[9]]
        aggregate = [(block * scale).T for block in blocks]
        columns = lambda ref, block: ref[:, block * channels : (block + 1) * channels].astype(jnp.float32)
        gate = jax.nn.sigmoid(dot_f32(aggregate[0], weight_gate_ref[...]))
        inner = dot_f32(aggregate[0], weight_scalar_ref[...])
        inner_sigmoid = jax.nn.sigmoid(inner)
        vectors = dot_f32(jnp.concatenate(aggregate[1:4], axis=0), weight_vector_ref[...])
        tensors = dot_f32(jnp.concatenate(aggregate[4:9], axis=0), weight_tensor_ref[...])
        gate_v, gate_t = gate[:, :channels], gate[:, channels:]
        scalar_out = (columns(features_ref, 0) + inner * inner_sigmoid).astype(jnp.bfloat16)
        updated_ref[:, :channels] = scalar_out
        charge_ref[...] = dot_f32(weight_charge_ref[...], scalar_out.astype(jnp.float32), ((1,), (1,)))
        grad_v, grad_t = [], []
        gate_grad_v = jnp.zeros((atoms, channels), jnp.float32)
        gate_grad_t = jnp.zeros((atoms, channels), jnp.float32)
        for axis in range(3):
            value = vectors[axis * atoms : (axis + 1) * atoms]
            given = columns(cotangent_ref, 1 + axis)
            updated_ref[:, (1 + axis) * channels : (2 + axis) * channels] = (
                columns(features_ref, 1 + axis) + gate_v * value
            ).astype(jnp.bfloat16)
            gate_grad_v = gate_grad_v + given * value
            grad_v.append(given * gate_v)
        for block in range(5):
            value = tensors[block * atoms : (block + 1) * atoms]
            given = columns(cotangent_ref, 4 + block)
            updated_ref[:, (4 + block) * channels : (5 + block) * channels] = (gate_t * value).astype(
                jnp.bfloat16
            )
            gate_grad_t = gate_grad_t + given * value
            grad_t.append(given * gate_t)
        inner_grad = columns(cotangent_ref, 0) * (
            inner_sigmoid * (1.0 + inner * (1.0 - inner_sigmoid))
        )
        gate_grad = jnp.concatenate([gate_grad_v, gate_grad_t], axis=1) * (gate * (1.0 - gate))
        across = ((1,), (1,))
        grad_s = dot_f32(inner_grad, weight_scalar_ref[...], across)
        grad_s = grad_s + dot_f32(gate_grad, weight_gate_ref[...], across)
        grad_v = dot_f32(jnp.concatenate(grad_v, axis=0), weight_vector_ref[...], across)
        grad_t = dot_f32(jnp.concatenate(grad_t, axis=0), weight_tensor_ref[...], across)
        t00, t11, t01, t12, t02 = [grad_t[block * atoms : (block + 1) * atoms] for block in range(5)]
        third = (t00 + t11) * (1.0 / 3.0)
        pieces = [grad_s] + [grad_v[axis * atoms : (axis + 1) * atoms] for axis in range(3)]
        pieces += [t00 - third, t11 - third, -third, 0.5 * t01, 0.5 * t12, 0.5 * t02]
        for block in range(10):
            node_grad_ref[block] = (pieces[block] * scale).T


def backward_kernel(
    groups,
    hidden_ref,
    unit_ref,
    index_ref,
    node_grad_ref,
    weight_radial_ref,
    cotangent_ref,
    own_grad_ref,
    *rest,
):
    message_refs = rest[: len(groups)]
    weight_t_ref, radial_ref, grad_ref, total_ref = rest[len(groups) :]
    step = pl.program_id(0)
    atoms = index_ref.shape[1]
    slots = index_ref.shape[0]
    channels = node_grad_ref.shape[1]
    table_rows = total_ref.shape[0]
    ghost = (table_rows - atoms) // 12

    @pl.when(step == 0)
    def _():
        load_radial_weight(weight_radial_ref, weight_t_ref)
        total_ref[...] = jnp.zeros_like(total_ref)

    radial_ref[...] = dot_t(weight_t_ref[...], hidden_ref[...], ((1,), (0,)))

    def group(number, carry):
        row = pl.multiple_of(number * ROW_GROUP, ROW_GROUP)
        node = [node_grad_ref[block, pl.ds(row, ROW_GROUP), :] for block in range(10)]
        g_s, g_v, diag, off = node[0], node[1:4], node[4:7], {(0, 1): node[7], (1, 2): node[8], (0, 2): node[9]}
        for slot in range(slots):
            lanes = slice(slot * atoms, (slot + 1) * atoms)
            unit = [unit_ref[axis, slot : slot + 1, :] for axis in range(3)]
            paths = [radial_ref[pl.ds(path * channels + row, ROW_GROUP), lanes] for path in range(7)]
            along = unit[0] * g_v[0] + unit[1] * g_v[1] + unit[2] * g_v[2]
            bent = [
                unit[0] * diag[0] + unit[1] * off[0, 1] + unit[2] * off[0, 2],
                unit[0] * off[0, 1] + unit[1] * diag[1] + unit[2] * off[1, 2],
                unit[0] * off[0, 2] + unit[1] * off[1, 2] + unit[2] * diag[2],
            ]
            twice = unit[0] * bent[0] + unit[1] * bent[1] + unit[2] * bent[2]
            scalar = paths[0] * g_s + paths[2] * along + paths[5] * twice
            pushed = paths[1] * g_s + paths[4] * along
            grad_ref[pl.ds(row, ROW_GROUP), lanes] = scalar.astype(jnp.bfloat16)
            for axis in range(3):
                vector = unit[axis] * pushed + paths[3] * g_v[axis] + paths[6] * bent[axis]
                grad_ref[pl.ds((1 + axis) * channels + row, ROW_GROUP), lanes] = vector.astype(jnp.bfloat16)
        return carry

    lax.fori_loop(0, channels // ROW_GROUP, group, 0)
    total_ref[...] += dot_t(sender_onehot(index_ref, table_rows), grad_ref[...], ((1,), (1,)))

    @pl.when(step == pl.num_programs(0) - 1)
    def _():
        own_grad_ref[...] = total_ref[:atoms, :] + cotangent_ref[:, : 4 * channels].astype(jnp.float32)
        for (_, cells), message_ref in zip(groups, message_refs):
            for place, cell in enumerate(cells):
                lower = atoms + cell * ghost
                message_ref[place * ghost : (place + 1) * ghost, :] = total_ref[
                    lower : lower + ghost, :
                ].astype(jnp.bfloat16)


def gather_kernel(groups, quad_ref, own_ref, *rest):
    message_refs, out_ref = rest[: len(groups)], rest[len(groups)]
    atoms = own_ref.shape[0]
    ghost = quad_ref.shape[3]
    rows = lax.broadcasted_iota(jnp.int32, (atoms, ghost), 0)
    total = own_ref[...]
    for (_, cells), message_ref in zip(groups, message_refs):
        for place, cell in enumerate(cells):
            row, col = QUARTER[BORDER[cell][0]], QUARTER[BORDER[cell][1]]
            chosen = (rows == quad_ref[0, row, col : col + 1, :]).astype(jnp.bfloat16)
            total = total + dot_t(chosen, message_ref[place * ghost : (place + 1) * ghost, :], ((1,), (0,)))
    out_ref[...] = total


def whole(shape):
    return pl.BlockSpec(shape, lambda step: (0,) * len(shape))


def for_sending(array):
    return jax.tree.map(lambda a: a.astype(jnp.bfloat16) if a.dtype == jnp.float32 else a, array)


def passed_along(value, axis, steps):
    count = lax.axis_size(axis)
    pairs = [(source, (source + steps) % count) for source in range(count)]
    return lax.ppermute(value, axis, pairs)


def spline_weights(offset):
    return (
        0.5 * (0.5 - offset) * (0.5 - offset),
        0.75 - offset * offset,
        0.5 * (0.5 + offset) * (0.5 + offset),
    )


def spline_table(base_cell, offset, points, wrapped):
    positions = jnp.arange(points, dtype=jnp.int32)[None, :]
    summed = jnp.zeros((base_cell.shape[0], points), jnp.float32)
    for step_id, weight in zip((-1, 0, 1), spline_weights(offset)):
        if wrapped:
            target = (base_cell + step_id) % points
        else:
            target = base_cell + step_id + 1
        summed = summed + weight[:, None] * (positions == target[:, None]).astype(jnp.float32)
    return summed


def influence(index_x, index_y, index_z, points_x, points_y, points_z):
    summed = 0.0
    correct = 1.0
    for index_k, points in ((index_x, points_x), (index_y, points_y), (index_z, points_z)):
        folded = jnp.minimum(index_k, points - index_k).astype(jnp.float32) / points
        modulus = 0.75 + 0.25 * jnp.cos(2.0 * jnp.pi / points * index_k.astype(jnp.float32))
        summed = summed + folded * folded
        correct = correct / (modulus * modulus)
    nonzero = summed > 0.0
    safe_sum = jnp.where(nonzero, summed, 1.0)
    value = COUPLING * jnp.exp(-2.0 * jnp.pi * jnp.pi * SMEAR * SMEAR * summed) / safe_sum * correct
    return jnp.where(nonzero, value, 0.0)


def hartley(points):
    positions = jnp.arange(points, dtype=jnp.int32)
    phase = positions[:, None] * positions[None, :] % points
    angle = phase.astype(jnp.float32) * (2.0 * jnp.pi / points)
    return jnp.cos(angle) + jnp.sin(angle)


def solve_potential(charge_grid, cells_x, cells_y, cells_z):
    full_x = cells_x * lax.axis_size("brick")
    full_y = cells_y * lax.axis_size("pme")
    part_y = full_y // lax.axis_size("brick")
    part_z = cells_z // lax.axis_size("pme")
    table_x = hartley(full_x)
    table_y = hartley(full_y)
    table_z = hartley(cells_z)
    spectrum = jnp.dot(charge_grid.reshape(-1, cells_z), table_z, precision=PRECISE).reshape(
        cells_x, cells_y, cells_z
    )
    spectrum = lax.all_to_all(
        for_sending(spectrum), "pme", split_axis=2, concat_axis=1, tiled=True
    ).astype(spectrum.dtype)
    spectrum = jnp.einsum("xyz,yk->xkz", spectrum, table_y, precision=PRECISE)
    spectrum = lax.all_to_all(spectrum, "brick", split_axis=1, concat_axis=0, tiled=True)
    spectrum = jnp.dot(table_x, spectrum.reshape(full_x, -1), precision=PRECISE).reshape(
        full_x, part_y, part_z
    )
    index_x = jnp.arange(full_x, dtype=jnp.int32)[:, None, None]
    index_y = lax.axis_index("brick") * part_y + jnp.arange(part_y, dtype=jnp.int32)[None, :, None]
    index_z = lax.axis_index("pme") * part_z + jnp.arange(part_z, dtype=jnp.int32)[None, None, :]
    spectrum = spectrum * influence(index_x, index_y, index_z, full_x, full_y, cells_z)
    spectrum = jnp.dot(table_x, spectrum.reshape(full_x, -1), precision=PRECISE).reshape(
        full_x, part_y, part_z
    )
    spectrum = lax.all_to_all(spectrum, "brick", split_axis=0, concat_axis=1, tiled=True)
    spectrum = jnp.einsum("xyz,yk->xkz", spectrum, table_y, precision=PRECISE)
    spectrum = lax.all_to_all(spectrum, "pme", split_axis=1, concat_axis=2, tiled=True)
    spectrum = jnp.dot(spectrum.reshape(-1, cells_z), table_z, precision=PRECISE).reshape(
        cells_x, cells_y, cells_z
    )
    return spectrum * (1.0 / (full_x * full_y * cells_z))


def fold_grid(charge_patch, cells_x, cells_y):
    for shift_by in (1, -1):
        source_plane = cells_x + 1 if shift_by == 1 else 0
        target_plane = 1 if shift_by == 1 else cells_x
        arrived = passed_along(charge_patch[source_plane], "brick", shift_by)
        charge_patch = charge_patch.at[target_plane].add(arrived)
    for shift_by in (1, -1):
        source_line = cells_y + 1 if shift_by == 1 else 0
        target_line = 1 if shift_by == 1 else cells_y
        arrived = passed_along(charge_patch[1 : cells_x + 1, source_line], "pme", shift_by)
        charge_patch = charge_patch.at[1 : cells_x + 1, target_line].add(arrived)
    return charge_patch[1 : cells_x + 1, 1 : cells_y + 1]


def per_device(
    features,
    cotangent,
    neighbor_index,
    neighbor_count,
    edge_vector,
    quad_index,
    weight_basis,
    weight_radial,
    weight_scalar,
    weight_gate,
    weight_vector,
    weight_tensor,
    weight_charge,
    grid_base,
    grid_frac,
):
    atoms, width = features.shape
    channels = width // 4
    slots = neighbor_index.shape[0] // atoms
    ghost = quad_index.shape[3]
    table_rows = atoms + 12 * ghost
    hidden_units = weight_basis.shape[1]
    groups = halo_groups(lax.axis_size("brick"), lax.axis_size("pme"))
    message_shapes = [
        jax.ShapeDtypeStruct((len(cells) * ghost, width), jnp.bfloat16) for _, cells in groups
    ]

    outgoing = pl.pallas_call(
        functools.partial(pack_kernel, groups), out_shape=message_shapes, name="pack"
    )(quad_index, features)
    incoming = [shifted(value, *steps) for (steps, _), value in zip(groups, outgoing)]

    index_t = neighbor_index.reshape(atoms, slots).T
    vector_t = edge_vector.reshape(3, atoms, slots).transpose(0, 2, 1)
    hidden, unit = pl.pallas_call(
        radial_kernel,
        out_shape=[
            jax.ShapeDtypeStruct((hidden_units, slots * atoms), jnp.bfloat16),
            jax.ShapeDtypeStruct((3, slots, atoms), jnp.float32),
        ],
        scratch_shapes=[pltpu.VMEM((weight_basis.shape[0], slots * atoms), jnp.float32)],
        compiler_params=params(),
        name="radial",
    )(vector_t, neighbor_count.reshape(1, atoms), weight_basis)

    block = SLOT_BLOCK * atoms
    edge_specs = [
        pl.BlockSpec((hidden_units, block), lambda step: (0, step)),
        pl.BlockSpec((3, SLOT_BLOCK, atoms), lambda step: (0, step, 0)),
        pl.BlockSpec((SLOT_BLOCK, atoms), lambda step: (step, 0)),
    ]
    weights = (weight_radial, weight_scalar, weight_gate, weight_vector, weight_tensor)
    charge_weight = weight_charge.reshape(1, channels)
    forward_shapes = [
        jax.ShapeDtypeStruct((atoms, 9 * channels), jnp.bfloat16),
        jax.ShapeDtypeStruct((1, atoms), jnp.float32),
        jax.ShapeDtypeStruct((10, channels, atoms), jnp.float32),
    ]
    updated, charge, node_grad = pl.pallas_call(
        functools.partial(forward_kernel, groups),
        grid=(slots // SLOT_BLOCK,),
        in_specs=edge_specs
        + [whole(features.shape)]
        + [whole(w.shape) for w in weights]
        + [whole(charge_weight.shape), whole(cotangent.shape)]
        + [whole(shape.shape) for shape in message_shapes],
        out_specs=[whole(shape.shape) for shape in forward_shapes],
        out_shape=forward_shapes,
        scratch_shapes=[
            pltpu.VMEM((table_rows, width), jnp.bfloat16),
            pltpu.VMEM((width, table_rows), jnp.bfloat16),
            pltpu.VMEM((7 * channels, hidden_units), jnp.bfloat16),
            pltpu.VMEM((7 * channels, block), jnp.float32),
            pltpu.VMEM((width, block), jnp.float32),
            pltpu.VMEM((10, channels, atoms), jnp.float32),
        ],
        compiler_params=params(),
        name="forward",
    )(hidden, unit, index_t, features, *weights, charge_weight, cotangent, *incoming)
    charge = charge.reshape(atoms)

    own_grad, *ghost_grads = pl.pallas_call(
        functools.partial(backward_kernel, groups),
        grid=(slots // SLOT_BLOCK,),
        in_specs=edge_specs
        + [whole((10, channels, atoms)), whole(weight_radial.shape), whole(cotangent.shape)],
        out_specs=[whole((atoms, width))] + [whole(shape.shape) for shape in message_shapes],
        out_shape=[jax.ShapeDtypeStruct((atoms, width), jnp.float32)] + message_shapes,
        scratch_shapes=[
            pltpu.VMEM((7 * channels, hidden_units), jnp.bfloat16),
            pltpu.VMEM((7 * channels, block), jnp.float32),
            pltpu.VMEM((width, block), jnp.bfloat16),
            pltpu.VMEM((table_rows, width), jnp.float32),
        ],
        compiler_params=params(),
        name="backward",
    )(hidden, unit, index_t, node_grad, weight_radial, cotangent)
    returned = [shifted(value, -steps[0], -steps[1]) for (steps, _), value in zip(groups, ghost_grads)]
    feature_grad = pl.pallas_call(
        functools.partial(gather_kernel, groups),
        out_shape=jax.ShapeDtypeStruct((atoms, width), jnp.float32),
        name="gather",
    )(quad_index, own_grad, *returned)

    cells_x = GX
    cells_y = GY
    cells_z = NGZ
    table_x = spline_table(grid_base[0], grid_frac[0], cells_x + 2, False)
    table_y = spline_table(grid_base[1], grid_frac[1], cells_y + 2, False)
    table_z = spline_table(grid_base[2], grid_frac[2], cells_z, True)
    plane_rows = (table_x[:, :, None] * table_y[:, None, :] * charge[:, None, None]).reshape(
        atoms, -1
    )
    spread_grid = lax.dot_general(plane_rows, table_z, (((0,), (0,)), ((), ())), precision=PRECISE)
    charge_patch = spread_grid.reshape(cells_x + 2, cells_y + 2, cells_z)
    charge_grid = fold_grid(charge_patch, cells_x, cells_y)
    potential = solve_potential(charge_grid, cells_x, cells_y, cells_z)
    return (updated, feature_grad, potential)


def solution(mesh):
    placed = (
        P(("brick", "pme"), None),
        P(("brick", "pme"), None),
        P(("brick", "pme")),
        P(("brick", "pme")),
        P(None, ("brick", "pme")),
        P(("brick", "pme"), None, None, None),
        P(),
        P(),
        P(),
        P(),
        P(),
        P(),
        P(),
        P(None, ("brick", "pme")),
        P(None, ("brick", "pme")),
    )
    return jax.shard_map(
        per_device,
        mesh=mesh,
        in_specs=placed,
        out_specs=(P(("brick", "pme"), None), P(("brick", "pme"), None), P("brick", "pme", None)),
        check_vma=False,
    )
```

```python
import functools
import itertools
import math

import jax
import jax.numpy as jnp
import ml_dtypes
import numpy as np
from jax import lax
from jax.experimental import pallas as pl
from jax.experimental.pallas import tpu as pltpu
from jax.sharding import PartitionSpec as P

GX = 6
GY = 24
NGZ = 192

CUTOFF = 5.0
SMEAR = 1.0
COUPLING = 0.1
PRECISE = lax.Precision.HIGHEST
BORDER = ((0, 0), (0, 1), (0, 2), (0, 3), (1, 0), (1, 3), (2, 0), (2, 3), (3, 0), (3, 1), (3, 2), (3, 3))
SHIFT = (-1, 0, 0, 1)
QUARTER = (1, 0, 1, 0)
SLOT_BLOCK = 4
WORK = jnp.bfloat16
ROW_GROUP = 16
PIECE = 128
VMEM_LIMIT = 48 * 1024 * 1024


def halo_groups(brick_count, pme_count):
    groups = {}
    for cell, (row, col) in enumerate(BORDER):
        step = (SHIFT[row] % brick_count, SHIFT[col] % pme_count)
        groups.setdefault(step, []).append(cell)
    return tuple((step, tuple(cells)) for step, cells in groups.items())


def shifted(value, brick_step, pme_step):
    bricks, pmes = lax.axis_size("brick"), lax.axis_size("pme")
    pairs = []
    for b in range(bricks):
        for p in range(pmes):
            source = (b + brick_step) % bricks * pmes + (p + pme_step) % pmes
            pairs.append((source, b * pmes + p))
    return lax.ppermute(value, ("brick", "pme"), pairs)


def dot_t(left, right, dims, precision=None):
    return lax.dot_general(
        left, right, (dims, ((), ())), precision=precision, preferred_element_type=jnp.float32
    )


def dot_f32(left, right, dims=((1,), (0,))):
    return dot_t(left, right, dims, PRECISE)


def params(**kwargs):
    return pltpu.CompilerParams(vmem_limit_bytes=VMEM_LIMIT, **kwargs)


def pack_kernel(groups, quad_ref, features_ref, *message_refs):
    atoms = features_ref.shape[0]
    ghost = quad_ref.shape[3]
    rows = lax.broadcasted_iota(jnp.int32, (atoms, ghost), 0)
    picked = {}
    for row in range(2):
        for col in range(2):
            chosen = (rows == quad_ref[0, row, col : col + 1, :]).astype(jnp.bfloat16)
            picked[row, col] = dot_t(chosen, features_ref[...], ((0,), (0,))).astype(jnp.bfloat16)
    for (_, cells), message_ref in zip(groups, message_refs):
        for place, cell in enumerate(cells):
            row, col = BORDER[cell]
            message_ref[place * ghost : (place + 1) * ghost, :] = picked[QUARTER[row], QUARTER[col]]


def radial_kernel(
    vector_ref,
    count_ref,
    basis_weight_ref,
    weight_radial_ref,
    features_ref,
    hidden_ref,
    unit_ref,
    weight_t_ref,
    features_t_ref,
    basis_ref,
):
    load_radial_weight(weight_radial_ref, weight_t_ref)
    transpose_into(features_t_ref, features_ref)
    slots, atoms = vector_ref.shape[1:]
    orders = basis_weight_ref.shape[0]
    parts = [vector_ref[axis] for axis in range(3)]
    distance = jnp.sqrt(parts[0] * parts[0] + parts[1] * parts[1] + parts[2] * parts[2])
    inverse = 1.0 / distance
    for axis in range(3):
        unit_ref[axis] = parts[axis] * inverse
    theta = distance * (math.pi / CUTOFF)
    cosine = jnp.cos(theta)
    live = lax.broadcasted_iota(jnp.int32, (slots, atoms), 0) < count_ref[...]
    envelope = jnp.where(live, 0.5 * (cosine + 1.0), 0.0)
    before = jnp.zeros_like(theta)
    current = jnp.sin(theta) * envelope
    for order in range(orders):
        for slot in range(slots):
            basis_ref[order : order + 1, slot * atoms : (slot + 1) * atoms] = current[slot : slot + 1, :]
        before, current = current, 2.0 * cosine * current - before
    width = 8 * atoms
    for start in range(0, slots * atoms, width):
        inner = dot_f32(basis_weight_ref[...], basis_ref[:, start : start + width], ((0,), (0,)))
        hidden_ref[:, start : start + width] = (inner * jax.nn.sigmoid(inner)).astype(jnp.bfloat16)


def load_radial_weight(weight_ref, weight_t_ref):
    channels = weight_ref.shape[1] // 7
    for path in range(7):
        block = weight_ref[:, path * channels : (path + 1) * channels].astype(jnp.float32)
        if path == 3:
            block = block - weight_ref[:, 4 * channels : 5 * channels].astype(jnp.float32) * (1.0 / 3.0)
        weight_t_ref[path * channels : (path + 1) * channels, :] = block.T.astype(jnp.bfloat16)


def transpose_into(out_ref, rows_ref):
    for lower in range(0, out_ref.shape[0], 128):
        out_ref[lower : lower + 128, :] = (
            rows_ref[:, lower : lower + 128].astype(jnp.float32).T.astype(jnp.bfloat16)
        )


def sender_onehot(index_ref, first, slots, table_rows):
    rows = lax.broadcasted_iota(jnp.int32, (table_rows, index_ref.shape[1]), 0)
    return jnp.concatenate(
        [(rows == index_ref[pl.ds(first + slot, 1), :]).astype(jnp.bfloat16) for slot in range(slots)], axis=1
    )


def unit_rows(unit_ref, first, slot):
    shape = (ROW_GROUP, unit_ref.shape[2])
    rows = [unit_ref[axis, pl.ds(first + slot, 1), :] for axis in range(3)]
    return [jnp.broadcast_to(row, shape).astype(WORK) for row in rows]


def tree_sum(terms):
    while len(terms) > 1:
        terms = [sum(terms[i + 1 : i + 2], terms[i]) for i in range(0, len(terms), 2)]
    return terms[0]


def radial_rows(radial_ref, weight_t_ref, hidden_ref, first, slots, atoms):
    for lower in range(0, slots, 2):
        lanes = pl.ds(pl.multiple_of((first + lower) * atoms, 2 * atoms), 2 * atoms)
        hidden = hidden_ref[:, lanes]
        for row in range(0, radial_ref.shape[0], PIECE):
            radial_ref[row : row + PIECE, lower * atoms : (lower + 2) * atoms] = dot_t(
                weight_t_ref[row : row + PIECE, :], hidden, ((1,), (0,))
            ).astype(WORK)
            yield


def interleave(vector_steps, matrix_steps):
    vector_steps, matrix_steps = iter(vector_steps), iter(matrix_steps)
    done = object()
    going = True
    while going:
        going = next(vector_steps, done) is not done
        for _ in range(3):
            going = (next(matrix_steps, done) is not done) or going


def layer_kernel(
    groups,
    hidden_ref,
    unit_ref,
    index_ref,
    weight_t_ref,
    features_t_ref,
    features_ref,
    weight_scalar_ref,
    weight_gate_ref,
    weight_vector_ref,
    weight_tensor_ref,
    weight_charge_ref,
    cotangent_ref,
    grid_base_ref,
    grid_frac_ref,
    *rest,
):
    count = len(groups)
    message_refs = rest[:count]
    updated_ref, charge_ref, own_grad_ref, *back_refs = rest[count : 2 * count + 3]
    (
        ghosts_ref,
        table_t_ref,
        chosen_ref,
        radial_even,
        radial_odd,
        sender_a,
        sender_b,
        total_ref,
        node_grad_ref,
        grad_a,
        grad_b,
        table_grad_ref,
    ) = rest[2 * count + 3 :]
    atoms, width = features_ref.shape
    channels = width // 4
    ghost = ghosts_ref.shape[0] // 12
    table_rows = table_t_ref.shape[1]
    slots = SLOT_BLOCK
    blocks = index_ref.shape[0] // slots
    steps = blocks // 2

    def products(block, radial_ref, sender_ref):
        first = block * slots
        yield from radial_rows(radial_ref, weight_t_ref, hidden_ref, first, slots, atoms)
        for lower in range(0, slots, 2):
            chosen = sender_onehot(index_ref, first + lower, 2, table_rows)
            chosen_ref[block, :, lower * atoms : (lower + 2) * atoms] = chosen
            for row in range(0, width, PIECE):
                sender_ref[row : row + PIECE, lower * atoms : (lower + 2) * atoms] = dot_t(
                    table_t_ref[row : row + PIECE, :], chosen, ((1,), (0,))
                ).astype(WORK)
                yield

    def messages(block, radial_ref, sender_ref):
        first = block * slots
        units = [unit_rows(unit_ref, first, slot) for slot in range(slots)]
        for row in range(0, channels, ROW_GROUP):
            terms = [[] for _ in range(10)]
            for slot in range(slots):
                lanes = slice(slot * atoms, (slot + 1) * atoms)
                unit = units[slot]
                paths = [
                    radial_ref[path * channels + row : path * channels + row + ROW_GROUP, lanes]
                    for path in range(7)
                ]
                scalar, *vector = [
                    sender_ref[part * channels + row : part * channels + row + ROW_GROUP, lanes]
                    for part in range(4)
                ]
                along = unit[0] * vector[0] + unit[1] * vector[1] + unit[2] * vector[2]
                terms[0].append(paths[0] * scalar + paths[1] * along)
                pushed = paths[2] * scalar + paths[4] * along
                twisted = paths[5] * scalar
                mixed = []
                for axis in range(3):
                    terms[1 + axis].append(unit[axis] * pushed + paths[3] * vector[axis])
                    mixed.append(unit[axis] * twisted + paths[6] * vector[axis])
                    terms[4 + axis].append(unit[axis] * mixed[axis])
                for place, (left, right) in enumerate(((0, 1), (1, 2), (0, 2))):
                    terms[7 + place].append(unit[left] * mixed[right] + unit[right] * mixed[left])
            for number in range(10):
                total_ref[number, row : row + ROW_GROUP, :] += tree_sum(terms[number]).astype(jnp.float32)
            yield

    for (_, cells), message_ref in zip(groups, message_refs):
        for place, cell in enumerate(cells):
            ghosts_ref[cell * ghost : (cell + 1) * ghost, :] = message_ref[
                place * ghost : (place + 1) * ghost, :
            ]
    table_t_ref[:, :atoms] = features_t_ref[...]
    transpose_into(table_t_ref.at[:, atoms:], ghosts_ref)
    total_ref[...] = jnp.zeros_like(total_ref)
    for _ in products(0, radial_even.at[0], sender_a):
        pass

    def forward_step(step, carry):
        interleave(
            messages(2 * step, radial_even.at[step], sender_a),
            products(2 * step + 1, radial_odd.at[step], sender_b),
        )
        following = jnp.minimum(2 * step + 2, blocks - 1)
        interleave(
            messages(2 * step + 1, radial_odd.at[step], sender_b),
            products(following, radial_even.at[step + 1], sender_a),
        )
        return carry

    lax.fori_loop(0, steps, forward_step, 0)
    scale = 1.0 / math.sqrt(index_ref.shape[0])
    trace = (total_ref[4] + total_ref[5] + total_ref[6]) * (1.0 / 3.0)
    sums = [total_ref[0], total_ref[1], total_ref[2], total_ref[3]]
    sums += [total_ref[4] - trace, total_ref[5] - trace]
    sums += [0.5 * total_ref[7], 0.5 * total_ref[8], 0.5 * total_ref[9]]
    aggregate = [(block * scale).T for block in sums]
    columns = lambda ref, block: ref[:, block * channels : (block + 1) * channels].astype(jnp.float32)
    gate = jax.nn.sigmoid(dot_f32(aggregate[0], weight_gate_ref[...]))
    inner = dot_f32(aggregate[0], weight_scalar_ref[...])
    inner_sigmoid = jax.nn.sigmoid(inner)
    vectors = dot_f32(jnp.concatenate(aggregate[1:4], axis=0), weight_vector_ref[...])
    tensors = dot_f32(jnp.concatenate(aggregate[4:9], axis=0), weight_tensor_ref[...])
    gate_v, gate_t = gate[:, :channels], gate[:, channels:]
    scalar_out = (columns(features_ref, 0) + inner * inner_sigmoid).astype(jnp.bfloat16)
    updated_ref[:, :channels] = scalar_out
    charge = dot_f32(weight_charge_ref[...], scalar_out.astype(jnp.float32), ((1,), (1,)))
    base, own_lines = grid_base_ref[...], lax.axis_index("pme") * GY
    rows = [charge, base[0:1], base[1:2] + own_lines, base[2:3], grid_frac_ref[...], jnp.zeros_like(charge)]
    rows = jnp.concatenate([row.astype(jnp.float32) for row in rows], axis=0)
    for device in range(charge_ref.shape[0]):
        charge_ref[device] = rows
    grad_v, grad_t = [], []
    gate_grad_v = jnp.zeros((atoms, channels), jnp.float32)
    gate_grad_t = jnp.zeros((atoms, channels), jnp.float32)
    for axis in range(3):
        value = vectors[axis * atoms : (axis + 1) * atoms]
        given = columns(cotangent_ref, 1 + axis)
        updated_ref[:, (1 + axis) * channels : (2 + axis) * channels] = (
            columns(features_ref, 1 + axis) + gate_v * value
        ).astype(jnp.bfloat16)
        gate_grad_v = gate_grad_v + given * value
        grad_v.append(given * gate_v)
    for block in range(5):
        value = tensors[block * atoms : (block + 1) * atoms]
        given = columns(cotangent_ref, 4 + block)
        updated_ref[:, (4 + block) * channels : (5 + block) * channels] = (gate_t * value).astype(
            jnp.bfloat16
        )
        gate_grad_t = gate_grad_t + given * value
        grad_t.append(given * gate_t)
    inner_grad = columns(cotangent_ref, 0) * (
        inner_sigmoid * (1.0 + inner * (1.0 - inner_sigmoid))
    )
    gate_grad = jnp.concatenate([gate_grad_v, gate_grad_t], axis=1) * (gate * (1.0 - gate))
    across = ((1,), (1,))
    grad_s = dot_f32(inner_grad, weight_scalar_ref[...], across)
    grad_s = grad_s + dot_f32(gate_grad, weight_gate_ref[...], across)
    grad_v = dot_f32(jnp.concatenate(grad_v, axis=0), weight_vector_ref[...], across)
    grad_t = dot_f32(jnp.concatenate(grad_t, axis=0), weight_tensor_ref[...], across)
    t00, t11, t01, t12, t02 = [grad_t[block * atoms : (block + 1) * atoms] for block in range(5)]
    third = (t00 + t11) * (1.0 / 3.0)
    pieces = [grad_s] + [grad_v[axis * atoms : (axis + 1) * atoms] for axis in range(3)]
    pieces += [t00 - third, t11 - third, -third, 0.5 * t01, 0.5 * t12, 0.5 * t02]
    for block in range(10):
        node_grad_ref[block] = (pieces[block] * scale).T


    table_grad_ref[...] = jnp.zeros_like(table_grad_ref)
    grad_b[...] = jnp.zeros_like(grad_b)

    def collect(block, grad_ref):
        for lower in range(0, width, 2 * channels):
            table_grad_ref[:, lower : lower + 2 * channels] += dot_t(
                chosen_ref[block], grad_ref[lower : lower + 2 * channels, :], ((1,), (1,))
            )
            yield

    def gradients(block, radial_ref, grad_ref):
        first = block * slots
        units = [unit_rows(unit_ref, first, slot) for slot in range(slots)]
        for row in range(0, channels, ROW_GROUP):
            node = [node_grad_ref[number, row : row + ROW_GROUP, :].astype(WORK) for number in range(10)]
            g_s, g_v, diag = node[0], node[1:4], node[4:7]
            off_01, off_12, off_02 = node[7:10]
            for slot in range(slots):
                lanes = slice(slot * atoms, (slot + 1) * atoms)
                unit = units[slot]
                paths = [
                    radial_ref[path * channels + row : path * channels + row + ROW_GROUP, lanes]
                    for path in range(7)
                ]
                along = unit[0] * g_v[0] + unit[1] * g_v[1] + unit[2] * g_v[2]
                bent = [
                    unit[0] * diag[0] + unit[1] * off_01 + unit[2] * off_02,
                    unit[0] * off_01 + unit[1] * diag[1] + unit[2] * off_12,
                    unit[0] * off_02 + unit[1] * off_12 + unit[2] * diag[2],
                ]
                twice = unit[0] * bent[0] + unit[1] * bent[1] + unit[2] * bent[2]
                pushed = paths[1] * g_s + paths[4] * along
                parts = [paths[0] * g_s + paths[2] * along + paths[5] * twice]
                for axis in range(3):
                    parts.append(unit[axis] * pushed + paths[3] * g_v[axis] + paths[6] * bent[axis])
                for number, part in enumerate(parts):
                    lower = number * channels + row
                    grad_ref[lower : lower + ROW_GROUP, lanes] = part.astype(jnp.bfloat16)
            yield

    def backward_step(step, carry):
        before = jnp.maximum(2 * step - 1, 0)
        interleave(gradients(2 * step, radial_even.at[step], grad_a), collect(before, grad_b))
        interleave(gradients(2 * step + 1, radial_odd.at[step], grad_b), collect(2 * step, grad_a))
        return carry

    lax.fori_loop(0, steps, backward_step, 0)
    for _ in collect(blocks - 1, grad_b):
        pass
    own_grad_ref[...] = table_grad_ref[:atoms, :] + cotangent_ref[:, :width].astype(jnp.float32)
    for (_, cells), back_ref in zip(groups, back_refs):
        for place, cell in enumerate(cells):
            lower = atoms + cell * ghost
            back_ref[place * ghost : (place + 1) * ghost, :] = table_grad_ref[
                lower : lower + ghost, :
            ].astype(jnp.bfloat16)


def gather_kernel(groups, quad_ref, own_ref, _, *rest):
    message_refs, out_ref = rest[: len(groups)], rest[len(groups)]
    atoms = own_ref.shape[0]
    ghost = quad_ref.shape[3]
    rows = lax.broadcasted_iota(jnp.int32, (atoms, ghost), 0)
    total = own_ref[...]
    for (_, cells), message_ref in zip(groups, message_refs):
        for place, cell in enumerate(cells):
            row, col = QUARTER[BORDER[cell][0]], QUARTER[BORDER[cell][1]]
            chosen = (rows == quad_ref[0, row, col : col + 1, :]).astype(jnp.bfloat16)
            total = total + dot_t(chosen, message_ref[place * ghost : (place + 1) * ghost, :], ((1,), (0,)))
    out_ref[...] = total


def whole(shape):
    return pl.BlockSpec(shape, lambda step: (0,) * len(shape))


def split_f32(value):
    high = value.astype(jnp.bfloat16)
    return high, (value - high.astype(jnp.float32)).astype(jnp.bfloat16)


def split_np(value):
    high = value.astype(ml_dtypes.bfloat16)
    low = (value - high.astype(np.float64)).astype(ml_dtypes.bfloat16)
    return np.concatenate([high, low], axis=0)


def hartley_np(points):
    angle = 2.0 * np.pi / points * (np.outer(np.arange(points), np.arange(points)) % points)
    return np.cos(angle) + np.sin(angle)


def damping_np(points):
    index = np.arange(points)
    folded = np.minimum(index, points - index) / points
    modulus = 0.75 + 0.25 * np.cos(2.0 * np.pi / points * index)
    return folded**2, np.exp(-2.0 * np.pi**2 * SMEAR**2 * folded**2) / modulus**2


def grid_tables(bricks, cells_x, cells_y, full_y, cells_z):
    full_x = bricks * cells_x
    wave_x, wave_y, wave_z = hartley_np(full_x), hartley_np(full_y), hartley_np(cells_z)
    (square_x, damp_x), (_, damp_y), (square_z, damp_z) = map(damping_np, (full_x, full_y, cells_z))
    window = (np.arange(bricks)[:, None] * cells_x + np.arange(-1, cells_x + 1)[None, :]) % full_x
    own_x = np.zeros((bricks, cells_x + 2, full_x))
    own_x[:, :cells_x] = (wave_x * damp_x[None, :]).reshape(bricks, cells_x, full_x)
    own_x = np.concatenate([split_np(block) for block in own_x], axis=0)
    scale = COUPLING / (full_x * full_y * cells_z)
    return (
        split_np(wave_z),
        split_np(wave_y),
        split_np(wave_x[:, window.reshape(-1)]),
        own_x,
        (wave_y * damp_y[None, :]).astype(np.float32),
        (wave_z * damp_z[:, None] * scale).astype(np.float32),
        square_x.reshape(-1, 1).astype(np.float32),
        square_z.reshape(1, -1).astype(np.float32),
    )


def spline_rows(cells, base, offset, points):
    weights = (
        0.5 * (0.5 - offset) * (0.5 - offset),
        0.75 - offset * offset,
        0.5 * (0.5 + offset) * (0.5 + offset),
    )
    below, above = base - 1.0, base + 1.0
    if points:
        below = jnp.where(below < 0.0, below + points, below)
        above = jnp.where(above >= points, above - points, above)
    table = jnp.where(cells == above, weights[2], 0.0)
    table = jnp.where(cells == below, weights[0], table)
    return jnp.where(cells == base, weights[1], table)


def dot_split(left, right, dims=((1,), (0,))):
    rows = left.shape[0] // 2
    both = dot_t(left, right[0], dims)
    return both[:rows] + both[rows:] + dot_t(left[:rows], right[1], dims)


def cell_numbers(rows, lanes):
    return lax.broadcasted_iota(jnp.int32, (rows, lanes), 0).astype(jnp.float32)


def potential_kernel(
    cells_y,
    atoms_ref,
    wave_z_ref,
    wave_y_ref,
    wave_x_ref,
    own_x_ref,
    own_y_ref,
    own_z_ref,
    square_x_ref,
    square_z_ref,
    out_ref,
    shape_z_ref,
    lines_ref,
    square_ref,
    planes_ref,
):
    step = pl.program_id(0)
    bricks, pieces, _, piece_atoms = atoms_ref.shape
    atoms = pieces * piece_atoms
    cells_x, _, cells_z = out_ref.shape
    window = cells_x + 2
    full_y = planes_ref.shape[0]
    chunk = lines_ref.shape[0]

    @pl.when(step == 0)
    def _():
        square_ref[...] = square_x_ref[...] + square_z_ref[...]

        def tables(brick, carry):
            block = jnp.concatenate([atoms_ref[brick, piece] for piece in range(pieces)], axis=1)
            row = lambda number: block[number : number + 1, :]
            table = spline_rows(cell_numbers(cells_z, atoms), row(3), row(6), float(cells_z))
            high, low = split_f32(dot_split(wave_z_ref[...], split_f32(table)))
            shape_z_ref[brick, 0], shape_z_ref[brick, 1] = high, low
            return carry

        lax.fori_loop(0, bricks, tables, 0, unroll=4)

    first = step * chunk

    def spread(brick, carry):
        block = jnp.concatenate([atoms_ref[brick, piece] for piece in range(pieces)], axis=1)
        row = lambda number: block[number : number + 1, :]
        along_x = row(0) * spline_rows(cell_numbers(window, atoms) - 1.0, row(1), row(4), 0)
        table = spline_rows(cell_numbers(full_y, atoms), row(2), row(5), float(full_y))
        wave_y = jnp.concatenate(
            [wave_y_ref[pl.ds(pl.multiple_of(first + part, 16), chunk), :] for part in (0, full_y)], axis=0
        )
        along_y = dot_split(wave_y, split_f32(table))
        rows = jnp.concatenate([along_y[line : line + 1, :] * along_x for line in range(chunk)], axis=0)
        high, low = split_f32(rows)
        z_high, z_low = shape_z_ref[brick, 0], shape_z_ref[brick, 1]
        across = ((1,), (1,))
        grid = dot_t(high, z_high, across) + dot_t(high, z_low, across) + dot_t(low, z_high, across)
        lines_ref[:, pl.ds(pl.multiple_of(brick * window, window), window), :] = grid.reshape(
            chunk, window, cells_z
        )
        return carry

    lax.fori_loop(0, bricks, spread, 0, unroll=2)
    own = pl.multiple_of(lax.axis_index("brick") * (2 * window), 2 * window)

    def solve(line, carry):
        wave = dot_split(wave_x_ref[...], split_f32(lines_ref[line]))
        number = first + line
        height = jnp.minimum(number, full_y - number).astype(jnp.float32) * (1.0 / full_y)
        square = square_ref[...] + height * height
        wave = wave * jnp.where(square > 0.0, 1.0 / jnp.where(square > 0.0, square, 1.0), 0.0)
        planes_ref[number] = dot_split(own_x_ref[pl.ds(own, 2 * window), :], split_f32(wave))
        return carry

    lax.fori_loop(0, chunk, solve, 0, unroll=8)

    @pl.when(step == pl.num_programs(0) - 1)
    def _():
        along_y = own_y_ref[pl.ds(pl.multiple_of(lax.axis_index("pme") * cells_y, 8), cells_y), :]
        for plane in range(cells_x):
            lines = dot_f32(along_y, planes_ref[:, plane, :])
            out_ref[plane] = dot_f32(lines, own_z_ref[...])


def potential_block(gathered, cells_x, cells_y, cells_z):
    bricks, pieces, rows, piece_atoms = gathered.shape
    full_y = cells_y * pieces
    atoms = pieces * piece_atoms
    window = cells_x + 2
    tables = grid_tables(bricks, cells_x, cells_y, full_y, cells_z)
    chunk = full_y if full_y <= 48 else 16
    return pl.pallas_call(
        functools.partial(potential_kernel, cells_y),
        grid=(full_y // chunk,),
        in_specs=[whole(gathered.shape)] + [whole(table.shape) for table in tables],
        out_specs=whole((cells_x, cells_y, cells_z)),
        out_shape=jax.ShapeDtypeStruct((cells_x, cells_y, cells_z), jnp.float32),
        scratch_shapes=[
            pltpu.VMEM((bricks, 2, cells_z, atoms), jnp.bfloat16),
            pltpu.VMEM((chunk, bricks * window, cells_z), jnp.float32),
            pltpu.VMEM((bricks * cells_x, cells_z), jnp.float32),
            pltpu.VMEM((full_y, window, cells_z), jnp.float32),
        ],
        compiler_params=params(),
        cost_estimate=pl.CostEstimate(flops=2 * 10**10, bytes_accessed=10**7, transcendentals=0),
        name="potential",
    )(gathered, *[jnp.asarray(table) for table in tables])


def all_charges(copies):
    bricks, pmes = lax.axis_size("brick"), lax.axis_size("pme")
    arrived = lax.all_to_all(copies, ("brick", "pme"), split_axis=0, concat_axis=0, tiled=True)
    return arrived.reshape(bricks, pmes, *copies.shape[1:])


def per_device(
    features,
    cotangent,
    neighbor_index,
    neighbor_count,
    edge_vector,
    quad_index,
    weight_basis,
    weight_radial,
    weight_scalar,
    weight_gate,
    weight_vector,
    weight_tensor,
    weight_charge,
    grid_base,
    grid_frac,
):
    atoms, width = features.shape
    channels = width // 4
    slots = neighbor_index.shape[0] // atoms
    ghost = quad_index.shape[3]
    table_rows = atoms + 12 * ghost
    hidden_units = weight_basis.shape[1]
    groups = halo_groups(lax.axis_size("brick"), lax.axis_size("pme"))
    message_shapes = [
        jax.ShapeDtypeStruct((len(cells) * ghost, width), jnp.bfloat16) for _, cells in groups
    ]

    outgoing = pl.pallas_call(
        functools.partial(pack_kernel, groups), out_shape=message_shapes, name="pack"
    )(quad_index, features)
    incoming = [shifted(value, *steps) for (steps, _), value in zip(groups, outgoing)]

    index_t = neighbor_index.reshape(atoms, slots).T
    vector_t = edge_vector.reshape(3, atoms, slots).transpose(0, 2, 1)
    hidden, unit, weight_t, features_t = pl.pallas_call(
        radial_kernel,
        out_shape=[
            jax.ShapeDtypeStruct((hidden_units, slots * atoms), jnp.bfloat16),
            jax.ShapeDtypeStruct((3, slots, atoms), jnp.float32),
            jax.ShapeDtypeStruct((7 * channels, hidden_units), jnp.bfloat16),
            jax.ShapeDtypeStruct((width, atoms), jnp.bfloat16),
        ],
        scratch_shapes=[pltpu.VMEM((weight_basis.shape[0], slots * atoms), jnp.float32)],
        compiler_params=params(),
        name="radial",
    )(vector_t, neighbor_count.reshape(1, atoms), weight_basis, weight_radial, features)

    block = SLOT_BLOCK * atoms
    steps = slots // (2 * SLOT_BLOCK)
    devices = lax.axis_size("brick") * lax.axis_size("pme")
    updated, charges, own_grad, *ghost_grads = pl.pallas_call(
        functools.partial(layer_kernel, groups),
        out_shape=[
            jax.ShapeDtypeStruct((atoms, 9 * channels), jnp.bfloat16),
            jax.ShapeDtypeStruct((devices, 8, atoms), jnp.float32),
            jax.ShapeDtypeStruct((atoms, width), jnp.float32),
        ]
        + message_shapes,
        scratch_shapes=[
            pltpu.VMEM((12 * ghost, width), jnp.bfloat16),
            pltpu.VMEM((width, table_rows), jnp.bfloat16),
            pltpu.VMEM((2 * steps, table_rows, block), jnp.bfloat16),
            pltpu.VMEM((steps + 1, 7 * channels, block), WORK),
            pltpu.VMEM((steps, 7 * channels, block), WORK),
            pltpu.VMEM((width, block), WORK),
            pltpu.VMEM((width, block), WORK),
            pltpu.VMEM((10, channels, atoms), jnp.float32),
            pltpu.VMEM((10, channels, atoms), jnp.float32),
            pltpu.VMEM((width, block), jnp.bfloat16),
            pltpu.VMEM((width, block), jnp.bfloat16),
            pltpu.VMEM((table_rows, width), jnp.float32),
        ],
        compiler_params=params(),
        name="layer",
    )(
        hidden,
        unit,
        index_t,
        weight_t,
        features_t,
        features,
        weight_scalar,
        weight_gate,
        weight_vector,
        weight_tensor,
        weight_charge.reshape(1, channels),
        cotangent,
        grid_base,
        grid_frac,
        *incoming,
    )
    gathered = all_charges(charges)
    potential = potential_block(gathered, GX, GY, NGZ)
    returned = [shifted(value, -steps[0], -steps[1]) for (steps, _), value in zip(groups, ghost_grads)]
    feature_grad = pl.pallas_call(
        functools.partial(gather_kernel, groups),
        in_specs=[pl.BlockSpec(memory_space=pltpu.VMEM)] * 2
        + [pl.BlockSpec(memory_space=pl.ANY)]
        + [pl.BlockSpec(memory_space=pltpu.VMEM)] * len(groups),
        out_shape=jax.ShapeDtypeStruct((atoms, width), jnp.float32),
        name="gather",
    )(quad_index, own_grad, potential, *returned)

    return (updated, feature_grad, potential)


def solution(mesh):
    placed = (
        P(("brick", "pme"), None),
        P(("brick", "pme"), None),
        P(("brick", "pme")),
        P(("brick", "pme")),
        P(None, ("brick", "pme")),
        P(("brick", "pme"), None, None, None),
        P(),
        P(),
        P(),
        P(),
        P(),
        P(),
        P(),
        P(None, ("brick", "pme")),
        P(None, ("brick", "pme")),
    )
    return jax.shard_map(
        per_device,
        mesh=mesh,
        in_specs=placed,
        out_specs=(P(("brick", "pme"), None), P(("brick", "pme"), None), P("brick", "pme", None)),
        check_vma=False,
    )
```

```python
import functools
import itertools
import math

import jax
import jax.numpy as jnp
import ml_dtypes
import numpy as np
from jax import lax
from jax.experimental import pallas as pl
from jax.experimental.pallas import tpu as pltpu
from jax.sharding import PartitionSpec as P

GX = 6
GY = 24
NGZ = 192

CUTOFF = 5.0
SMEAR = 1.0
COUPLING = 0.1
PRECISE = lax.Precision.HIGHEST
BORDER = ((0, 0), (0, 1), (0, 2), (0, 3), (1, 0), (1, 3), (2, 0), (2, 3), (3, 0), (3, 1), (3, 2), (3, 3))
SHIFT = (-1, 0, 0, 1)
QUARTER = (1, 0, 1, 0)
SLOT_BLOCK = 8
WORK = jnp.bfloat16
ROW_GROUP = 16
PIECE = 128
LINES = 8
SOLVE_UNROLL = 1
VMEM_LIMIT = 48 * 1024 * 1024


def halo_groups(brick_count, pme_count):
    groups = {}
    for cell, (row, col) in enumerate(BORDER):
        step = (SHIFT[row] % brick_count, SHIFT[col] % pme_count)
        groups.setdefault(step, []).append(cell)
    return tuple((step, tuple(cells)) for step, cells in groups.items())


def shifted(value, brick_step, pme_step):
    bricks, pmes = lax.axis_size("brick"), lax.axis_size("pme")
    pairs = []
    for b in range(bricks):
        for p in range(pmes):
            source = (b + brick_step) % bricks * pmes + (p + pme_step) % pmes
            pairs.append((source, b * pmes + p))
    return lax.ppermute(value, ("brick", "pme"), pairs)


def dot_t(left, right, dims, precision=None):
    return lax.dot_general(
        left, right, (dims, ((), ())), precision=precision, preferred_element_type=jnp.float32
    )


def dot_f32(left, right, dims=((1,), (0,))):
    return dot_t(left, right, dims, PRECISE)


def params(**kwargs):
    return pltpu.CompilerParams(vmem_limit_bytes=VMEM_LIMIT, **kwargs)


def pack_kernel(groups, quad_ref, features_ref, *message_refs):
    atoms = features_ref.shape[0]
    ghost = quad_ref.shape[3]
    rows = lax.broadcasted_iota(jnp.int32, (atoms, ghost), 0)
    picked = {}
    for row in range(2):
        for col in range(2):
            chosen = (rows == quad_ref[0, row, col : col + 1, :]).astype(jnp.bfloat16)
            picked[row, col] = dot_t(chosen, features_ref[...], ((0,), (0,))).astype(jnp.bfloat16)
    for (_, cells), message_ref in zip(groups, message_refs):
        for place, cell in enumerate(cells):
            row, col = BORDER[cell]
            message_ref[place * ghost : (place + 1) * ghost, :] = picked[QUARTER[row], QUARTER[col]]


def radial_kernel(
    vector_ref,
    count_ref,
    basis_weight_ref,
    weight_radial_ref,
    features_ref,
    hidden_ref,
    unit_ref,
    weight_t_ref,
    features_t_ref,
    basis_ref,
):
    load_radial_weight(weight_radial_ref, weight_t_ref)
    transpose_into(features_t_ref, features_ref)
    slots, atoms = vector_ref.shape[1:]
    orders = basis_weight_ref.shape[0]
    parts = [vector_ref[axis] for axis in range(3)]
    distance = jnp.sqrt(parts[0] * parts[0] + parts[1] * parts[1] + parts[2] * parts[2])
    inverse = 1.0 / distance
    for axis in range(3):
        unit_ref[axis] = parts[axis] * inverse
    theta = distance * (math.pi / CUTOFF)
    cosine = jnp.cos(theta)
    live = lax.broadcasted_iota(jnp.int32, (slots, atoms), 0) < count_ref[...]
    envelope = jnp.where(live, 0.5 * (cosine + 1.0), 0.0)
    before = jnp.zeros_like(theta)
    current = jnp.sin(theta) * envelope
    for order in range(orders):
        for slot in range(slots):
            basis_ref[order : order + 1, slot * atoms : (slot + 1) * atoms] = current[slot : slot + 1, :]
        before, current = current, 2.0 * cosine * current - before
    width = 8 * atoms
    for start in range(0, slots * atoms, width):
        inner = dot_f32(basis_weight_ref[...], basis_ref[:, start : start + width], ((0,), (0,)))
        hidden_ref[:, start : start + width] = (inner * jax.nn.sigmoid(inner)).astype(jnp.bfloat16)


def load_radial_weight(weight_ref, weight_t_ref):
    channels = weight_ref.shape[1] // 7
    for path in range(7):
        block = weight_ref[:, path * channels : (path + 1) * channels].astype(jnp.float32)
        if path == 3:
            block = block - weight_ref[:, 4 * channels : 5 * channels].astype(jnp.float32) * (1.0 / 3.0)
        weight_t_ref[path * channels : (path + 1) * channels, :] = block.T.astype(jnp.bfloat16)


def transpose_into(out_ref, rows_ref):
    for lower in range(0, out_ref.shape[0], 128):
        out_ref[lower : lower + 128, :] = (
            rows_ref[:, lower : lower + 128].astype(jnp.float32).T.astype(jnp.bfloat16)
        )


def sender_onehot(index_ref, first, slots, table_rows):
    rows = lax.broadcasted_iota(jnp.int32, (table_rows, index_ref.shape[1]), 0)
    return jnp.concatenate(
        [(rows == index_ref[pl.ds(first + slot, 1), :]).astype(jnp.bfloat16) for slot in range(slots)], axis=1
    )


def unit_rows(unit_ref, first, slot):
    shape = (ROW_GROUP, unit_ref.shape[2])
    rows = [unit_ref[axis, pl.ds(first + slot, 1), :] for axis in range(3)]
    return [jnp.broadcast_to(row, shape).astype(WORK) for row in rows]


def tree_sum(terms):
    while len(terms) > 1:
        terms = [sum(terms[i + 1 : i + 2], terms[i]) for i in range(0, len(terms), 2)]
    return terms[0]


def radial_rows(radial_ref, weight_t_ref, hidden_ref, first, slots, atoms):
    for lower in range(0, slots, 2):
        lanes = pl.ds(pl.multiple_of((first + lower) * atoms, 2 * atoms), 2 * atoms)
        hidden = hidden_ref[:, lanes]
        for row in range(0, radial_ref.shape[0], PIECE):
            radial_ref[row : row + PIECE, lower * atoms : (lower + 2) * atoms] = dot_t(
                weight_t_ref[row : row + PIECE, :], hidden, ((1,), (0,))
            ).astype(WORK)
            yield


def interleave(vector_steps, matrix_steps):
    vector_steps, matrix_steps = iter(vector_steps), iter(matrix_steps)
    done = object()
    going = True
    while going:
        going = next(vector_steps, done) is not done
        for _ in range(3):
            going = (next(matrix_steps, done) is not done) or going


def layer_kernel(
    groups,
    hidden_ref,
    unit_ref,
    index_ref,
    weight_t_ref,
    features_t_ref,
    features_ref,
    weight_scalar_ref,
    weight_gate_ref,
    weight_vector_ref,
    weight_tensor_ref,
    weight_charge_ref,
    cotangent_ref,
    grid_base_ref,
    grid_frac_ref,
    *rest,
):
    count = len(groups)
    message_refs = rest[:count]
    updated_ref, charge_ref, own_grad_ref, *back_refs = rest[count : 2 * count + 3]
    (
        ghosts_ref,
        table_t_ref,
        chosen_ref,
        radial_even,
        radial_odd,
        sender_a,
        sender_b,
        total_ref,
        node_grad_ref,
        grad_a,
        grad_b,
        table_grad_ref,
    ) = rest[2 * count + 3 :]
    atoms, width = features_ref.shape
    channels = width // 4
    ghost = ghosts_ref.shape[0] // 12
    table_rows = table_t_ref.shape[1]
    slots = SLOT_BLOCK
    blocks = index_ref.shape[0] // slots
    steps = blocks // 2

    def products(block, radial_ref, sender_ref):
        first = block * slots
        yield from radial_rows(radial_ref, weight_t_ref, hidden_ref, first, slots, atoms)
        for lower in range(0, slots, 2):
            chosen = sender_onehot(index_ref, first + lower, 2, table_rows)
            chosen_ref[block, :, lower * atoms : (lower + 2) * atoms] = chosen
            for row in range(0, width, PIECE):
                sender_ref[row : row + PIECE, lower * atoms : (lower + 2) * atoms] = dot_t(
                    table_t_ref[row : row + PIECE, :], chosen, ((1,), (0,))
                ).astype(WORK)
                yield

    def messages(block, radial_ref, sender_ref):
        first = block * slots
        units = [unit_rows(unit_ref, first, slot) for slot in range(slots)]
        for row in range(0, channels, ROW_GROUP):
            terms = [[] for _ in range(10)]
            for slot in range(slots):
                lanes = slice(slot * atoms, (slot + 1) * atoms)
                unit = units[slot]
                paths = [
                    radial_ref[path * channels + row : path * channels + row + ROW_GROUP, lanes]
                    for path in range(7)
                ]
                scalar, *vector = [
                    sender_ref[part * channels + row : part * channels + row + ROW_GROUP, lanes]
                    for part in range(4)
                ]
                along = unit[0] * vector[0] + unit[1] * vector[1] + unit[2] * vector[2]
                terms[0].append(paths[0] * scalar + paths[1] * along)
                pushed = paths[2] * scalar + paths[4] * along
                twisted = paths[5] * scalar
                mixed = []
                for axis in range(3):
                    terms[1 + axis].append(unit[axis] * pushed + paths[3] * vector[axis])
                    mixed.append(unit[axis] * twisted + paths[6] * vector[axis])
                    terms[4 + axis].append(unit[axis] * mixed[axis])
                for place, (left, right) in enumerate(((0, 1), (1, 2), (0, 2))):
                    terms[7 + place].append(unit[left] * mixed[right] + unit[right] * mixed[left])
            for number in range(10):
                total_ref[number, row : row + ROW_GROUP, :] += tree_sum(terms[number]).astype(jnp.float32)
            yield

    for (_, cells), message_ref in zip(groups, message_refs):
        for place, cell in enumerate(cells):
            ghosts_ref[cell * ghost : (cell + 1) * ghost, :] = message_ref[
                place * ghost : (place + 1) * ghost, :
            ]
    table_t_ref[:, :atoms] = features_t_ref[...]
    transpose_into(table_t_ref.at[:, atoms:], ghosts_ref)
    total_ref[...] = jnp.zeros_like(total_ref)
    for _ in products(0, radial_even.at[0], sender_a):
        pass

    def forward_step(step, carry):
        interleave(
            messages(2 * step, radial_even.at[step], sender_a),
            products(2 * step + 1, radial_odd.at[step], sender_b),
        )
        following = jnp.minimum(2 * step + 2, blocks - 1)
        interleave(
            messages(2 * step + 1, radial_odd.at[step], sender_b),
            products(following, radial_even.at[step + 1], sender_a),
        )
        return carry

    lax.fori_loop(0, steps, forward_step, 0)
    scale = 1.0 / math.sqrt(index_ref.shape[0])
    trace = (total_ref[4] + total_ref[5] + total_ref[6]) * (1.0 / 3.0)
    sums = [total_ref[0], total_ref[1], total_ref[2], total_ref[3]]
    sums += [total_ref[4] - trace, total_ref[5] - trace]
    sums += [0.5 * total_ref[7], 0.5 * total_ref[8], 0.5 * total_ref[9]]
    aggregate = [(block * scale).T for block in sums]
    columns = lambda ref, block: ref[:, block * channels : (block + 1) * channels].astype(jnp.float32)
    gate = jax.nn.sigmoid(dot_f32(aggregate[0], weight_gate_ref[...]))
    inner = dot_f32(aggregate[0], weight_scalar_ref[...])
    inner_sigmoid = jax.nn.sigmoid(inner)
    vectors = dot_f32(jnp.concatenate(aggregate[1:4], axis=0), weight_vector_ref[...])
    tensors = dot_f32(jnp.concatenate(aggregate[4:9], axis=0), weight_tensor_ref[...])
    gate_v, gate_t = gate[:, :channels], gate[:, channels:]
    scalar_out = (columns(features_ref, 0) + inner * inner_sigmoid).astype(jnp.bfloat16)
    updated_ref[:, :channels] = scalar_out
    charge = dot_f32(weight_charge_ref[...], scalar_out.astype(jnp.float32), ((1,), (1,)))
    base, own_lines = grid_base_ref[...], lax.axis_index("pme") * GY
    rows = [charge, base[0:1], base[1:2] + own_lines, base[2:3], grid_frac_ref[...], jnp.zeros_like(charge)]
    rows = jnp.concatenate([row.astype(jnp.float32) for row in rows], axis=0)
    for device in range(charge_ref.shape[0]):
        charge_ref[device] = rows
    grad_v, grad_t = [], []
    gate_grad_v = jnp.zeros((atoms, channels), jnp.float32)
    gate_grad_t = jnp.zeros((atoms, channels), jnp.float32)
    for axis in range(3):
        value = vectors[axis * atoms : (axis + 1) * atoms]
        given = columns(cotangent_ref, 1 + axis)
        updated_ref[:, (1 + axis) * channels : (2 + axis) * channels] = (
            columns(features_ref, 1 + axis) + gate_v * value
        ).astype(jnp.bfloat16)
        gate_grad_v = gate_grad_v + given * value
        grad_v.append(given * gate_v)
    for block in range(5):
        value = tensors[block * atoms : (block + 1) * atoms]
        given = columns(cotangent_ref, 4 + block)
        updated_ref[:, (4 + block) * channels : (5 + block) * channels] = (gate_t * value).astype(
            jnp.bfloat16
        )
        gate_grad_t = gate_grad_t + given * value
        grad_t.append(given * gate_t)
    inner_grad = columns(cotangent_ref, 0) * (
        inner_sigmoid * (1.0 + inner * (1.0 - inner_sigmoid))
    )
    gate_grad = jnp.concatenate([gate_grad_v, gate_grad_t], axis=1) * (gate * (1.0 - gate))
    across = ((1,), (1,))
    grad_s = dot_f32(inner_grad, weight_scalar_ref[...], across)
    grad_s = grad_s + dot_f32(gate_grad, weight_gate_ref[...], across)
    grad_v = dot_f32(jnp.concatenate(grad_v, axis=0), weight_vector_ref[...], across)
    grad_t = dot_f32(jnp.concatenate(grad_t, axis=0), weight_tensor_ref[...], across)
    t00, t11, t01, t12, t02 = [grad_t[block * atoms : (block + 1) * atoms] for block in range(5)]
    third = (t00 + t11) * (1.0 / 3.0)
    pieces = [grad_s] + [grad_v[axis * atoms : (axis + 1) * atoms] for axis in range(3)]
    pieces += [t00 - third, t11 - third, -third, 0.5 * t01, 0.5 * t12, 0.5 * t02]
    for block in range(10):
        node_grad_ref[block] = (pieces[block] * scale).T


    table_grad_ref[...] = jnp.zeros_like(table_grad_ref)
    grad_b[...] = jnp.zeros_like(grad_b)

    def collect(block, grad_ref):
        for lower in range(0, width, 2 * channels):
            table_grad_ref[:, lower : lower + 2 * channels] += dot_t(
                chosen_ref[block], grad_ref[lower : lower + 2 * channels, :], ((1,), (1,))
            )
            yield

    def gradients(block, radial_ref, grad_ref):
        first = block * slots
        units = [unit_rows(unit_ref, first, slot) for slot in range(slots)]
        for row in range(0, channels, ROW_GROUP):
            node = [node_grad_ref[number, row : row + ROW_GROUP, :].astype(WORK) for number in range(10)]
            g_s, g_v, diag = node[0], node[1:4], node[4:7]
            off_01, off_12, off_02 = node[7:10]
            for slot in range(slots):
                lanes = slice(slot * atoms, (slot + 1) * atoms)
                unit = units[slot]
                paths = [
                    radial_ref[path * channels + row : path * channels + row + ROW_GROUP, lanes]
                    for path in range(7)
                ]
                along = unit[0] * g_v[0] + unit[1] * g_v[1] + unit[2] * g_v[2]
                bent = [
                    unit[0] * diag[0] + unit[1] * off_01 + unit[2] * off_02,
                    unit[0] * off_01 + unit[1] * diag[1] + unit[2] * off_12,
                    unit[0] * off_02 + unit[1] * off_12 + unit[2] * diag[2],
                ]
                twice = unit[0] * bent[0] + unit[1] * bent[1] + unit[2] * bent[2]
                pushed = paths[1] * g_s + paths[4] * along
                parts = [paths[0] * g_s + paths[2] * along + paths[5] * twice]
                for axis in range(3):
                    parts.append(unit[axis] * pushed + paths[3] * g_v[axis] + paths[6] * bent[axis])
                for number, part in enumerate(parts):
                    lower = number * channels + row
                    grad_ref[lower : lower + ROW_GROUP, lanes] = part.astype(jnp.bfloat16)
            yield

    def backward_step(step, carry):
        before = jnp.maximum(2 * step - 1, 0)
        interleave(gradients(2 * step, radial_even.at[step], grad_a), collect(before, grad_b))
        interleave(gradients(2 * step + 1, radial_odd.at[step], grad_b), collect(2 * step, grad_a))
        return carry

    lax.fori_loop(0, steps, backward_step, 0)
    for _ in collect(blocks - 1, grad_b):
        pass
    own_grad_ref[...] = table_grad_ref[:atoms, :] + cotangent_ref[:, :width].astype(jnp.float32)
    for (_, cells), back_ref in zip(groups, back_refs):
        for place, cell in enumerate(cells):
            lower = atoms + cell * ghost
            back_ref[place * ghost : (place + 1) * ghost, :] = table_grad_ref[
                lower : lower + ghost, :
            ].astype(jnp.bfloat16)


def gather_kernel(groups, quad_ref, own_ref, _, *rest):
    message_refs, out_ref = rest[: len(groups)], rest[len(groups)]
    atoms = own_ref.shape[0]
    ghost = quad_ref.shape[3]
    rows = lax.broadcasted_iota(jnp.int32, (atoms, ghost), 0)
    total = own_ref[...]
    for (_, cells), message_ref in zip(groups, message_refs):
        for place, cell in enumerate(cells):
            row, col = QUARTER[BORDER[cell][0]], QUARTER[BORDER[cell][1]]
            chosen = (rows == quad_ref[0, row, col : col + 1, :]).astype(jnp.bfloat16)
            total = total + dot_t(chosen, message_ref[place * ghost : (place + 1) * ghost, :], ((1,), (0,)))
    out_ref[...] = total


def whole(shape):
    return pl.BlockSpec(shape, lambda step: (0,) * len(shape))


def split_f32(value):
    high = value.astype(jnp.bfloat16)
    return high, (value - high.astype(jnp.float32)).astype(jnp.bfloat16)


def split_np(value):
    high = value.astype(ml_dtypes.bfloat16)
    low = (value - high.astype(np.float64)).astype(ml_dtypes.bfloat16)
    return np.concatenate([high, low], axis=0)


def hartley_np(points):
    angle = 2.0 * np.pi / points * (np.outer(np.arange(points), np.arange(points)) % points)
    return np.cos(angle) + np.sin(angle)


def damping_np(points):
    index = np.arange(points)
    folded = np.minimum(index, points - index) / points
    modulus = 0.75 + 0.25 * np.cos(2.0 * np.pi / points * index)
    return folded**2, np.exp(-2.0 * np.pi**2 * SMEAR**2 * folded**2) / modulus**2


def grid_tables(bricks, cells_x, cells_y, full_y, cells_z):
    full_x = bricks * cells_x
    wave_x, wave_y, wave_z = hartley_np(full_x), hartley_np(full_y), hartley_np(cells_z)
    (square_x, damp_x), (_, damp_y), (square_z, damp_z) = map(damping_np, (full_x, full_y, cells_z))
    window = (np.arange(bricks)[:, None] * cells_x + np.arange(-1, cells_x + 1)[None, :]) % full_x
    own_x = np.zeros((bricks, cells_x + 2, full_x))
    own_x[:, :cells_x] = (wave_x * damp_x[None, :]).reshape(bricks, cells_x, full_x)
    own_x = np.concatenate([split_np(block) for block in own_x], axis=0)
    scale = COUPLING / (full_x * full_y * cells_z)
    extra = -cells_z % 128
    tail = lambda value, fill, axis: np.pad(
        value, [(0, extra) if dim == axis else (0, 0) for dim in range(value.ndim)], constant_values=fill
    )
    square_z = tail(square_z, 1.0, 0)
    return (
        split_np(tail(wave_z, 0.0, 0)),
        split_np(wave_y),
        split_np(wave_x[:, window.reshape(-1)]),
        own_x,
        (wave_y * damp_y[None, :]).astype(np.float32),
        tail(wave_z * damp_z[:, None] * scale, 0.0, 0).astype(np.float32),
        square_x.reshape(-1, 1).astype(np.float32),
        square_z.reshape(1, -1).astype(np.float32),
    )


def spline_rows(cells, base, offset, points):
    weights = (
        0.5 * (0.5 - offset) * (0.5 - offset),
        0.75 - offset * offset,
        0.5 * (0.5 + offset) * (0.5 + offset),
    )
    below, above = base - 1.0, base + 1.0
    if points:
        below = jnp.where(below < 0.0, below + points, below)
        above = jnp.where(above >= points, above - points, above)
    table = jnp.where(cells == above, weights[2], 0.0)
    table = jnp.where(cells == below, weights[0], table)
    return jnp.where(cells == base, weights[1], table)


def dot_split(left, right, dims=((1,), (0,))):
    rows = left.shape[0] // 2
    both = dot_t(left, right[0], dims)
    return both[:rows] + both[rows:] + dot_t(left[:rows], right[1], dims)


def cell_numbers(rows, lanes):
    return lax.broadcasted_iota(jnp.int32, (rows, lanes), 0).astype(jnp.float32)


def potential_kernel(
    cells_y,
    atoms_ref,
    wave_z_ref,
    wave_y_ref,
    wave_x_ref,
    own_x_ref,
    own_y_ref,
    own_z_ref,
    square_x_ref,
    square_z_ref,
    out_ref,
    shape_z_ref,
    lines_ref,
    square_ref,
    planes_ref,
):
    step = pl.program_id(0)
    bricks, pieces, _, piece_atoms = atoms_ref.shape
    atoms = pieces * piece_atoms
    cells_x, _, cells_z = out_ref.shape
    window = cells_x + 2
    full_y = planes_ref.shape[0]
    lanes_z = square_ref.shape[1]
    chunk = lines_ref.shape[1] // lanes_z

    @pl.when(step == 0)
    def _():
        square_ref[...] = square_x_ref[...] + square_z_ref[...]

        def tables(brick, carry):
            block = jnp.concatenate([atoms_ref[brick, piece] for piece in range(pieces)], axis=1)
            row = lambda number: block[number : number + 1, :]
            table = spline_rows(cell_numbers(cells_z, atoms), row(3), row(6), float(cells_z))
            high, low = split_f32(dot_split(wave_z_ref[...], split_f32(table)))
            shape_z_ref[brick, 0], shape_z_ref[brick, 1] = high, low
            return carry

        lax.fori_loop(0, bricks, tables, 0, unroll=4)

    first = step * chunk

    def spread(brick, carry):
        block = jnp.concatenate([atoms_ref[brick, piece] for piece in range(pieces)], axis=1)
        row = lambda number: block[number : number + 1, :]
        along_x = row(0) * spline_rows(cell_numbers(window, atoms) - 1.0, row(1), row(4), 0)
        table = spline_rows(cell_numbers(full_y, atoms), row(2), row(5), float(full_y))
        wave_y = jnp.concatenate(
            [wave_y_ref[pl.ds(pl.multiple_of(first + part, 16), chunk), :] for part in (0, full_y)], axis=0
        )
        along_y = dot_split(wave_y, split_f32(table))
        rows = jnp.concatenate([along_y[line : line + 1, :] * along_x for line in range(chunk)], axis=0)
        high, low = split_f32(rows)
        z_high, z_low = shape_z_ref[brick, 0], shape_z_ref[brick, 1]
        across = ((1,), (1,))
        grid = dot_t(high, z_high, across) + dot_t(high, z_low, across) + dot_t(low, z_high, across)
        place = pl.ds(pl.multiple_of(brick * window, window), window)
        for line in range(chunk):
            lines_ref[place, line * lanes_z : (line + 1) * lanes_z] = grid[line * window : (line + 1) * window]
        return carry

    lax.fori_loop(0, bricks, spread, 0, unroll=2)
    own = pl.multiple_of(lax.axis_index("brick") * (2 * window), 2 * window)

    def solve(batch, carry):
        lanes = pl.ds(pl.multiple_of(batch * (LINES * lanes_z), LINES * lanes_z), LINES * lanes_z)
        wave = dot_split(wave_x_ref[...], split_f32(lines_ref[:, lanes]))
        squares = []
        for line in range(LINES):
            number = first + batch * LINES + line
            height = jnp.minimum(number, full_y - number).astype(jnp.float32) * (1.0 / full_y)
            squares.append(square_ref[...] + height * height)
        square = jnp.concatenate(squares, axis=1)
        inverse = pl.reciprocal(square, approx=True)
        inverse = inverse * (2.0 - square * inverse)
        wave = wave * jnp.where(square > 0.0, inverse, 0.0)
        planes = dot_split(own_x_ref[pl.ds(own, 2 * window), :], split_f32(wave))
        for line in range(LINES):
            planes_ref[first + batch * LINES + line] = planes[:, line * lanes_z : (line + 1) * lanes_z]
        return carry

    lax.fori_loop(0, chunk // LINES, solve, 0, unroll=SOLVE_UNROLL)

    @pl.when(step == pl.num_programs(0) - 1)
    def _():
        along_y = own_y_ref[pl.ds(pl.multiple_of(lax.axis_index("pme") * cells_y, 8), cells_y), :]
        lines = [dot_f32(along_y, planes_ref[:, plane, :]) for plane in range(cells_x)]
        block = dot_f32(jnp.concatenate(lines, axis=0), own_z_ref[...])
        out_ref[...] = block.reshape(cells_x, cells_y, cells_z)


def potential_block(gathered, cells_x, cells_y, cells_z):
    bricks, pieces, rows, piece_atoms = gathered.shape
    full_y = cells_y * pieces
    atoms = pieces * piece_atoms
    window = cells_x + 2
    tables = grid_tables(bricks, cells_x, cells_y, full_y, cells_z)
    chunk = full_y if full_y <= 48 else 16
    lanes_z = cells_z + -cells_z % 128
    return pl.pallas_call(
        functools.partial(potential_kernel, cells_y),
        grid=(full_y // chunk,),
        in_specs=[whole(gathered.shape)] + [whole(table.shape) for table in tables],
        out_specs=whole((cells_x, cells_y, cells_z)),
        out_shape=jax.ShapeDtypeStruct((cells_x, cells_y, cells_z), jnp.float32),
        scratch_shapes=[
            pltpu.VMEM((bricks, 2, lanes_z, atoms), jnp.bfloat16),
            pltpu.VMEM((bricks * window, chunk * lanes_z), jnp.float32),
            pltpu.VMEM((bricks * cells_x, lanes_z), jnp.float32),
            pltpu.VMEM((full_y, window, lanes_z), jnp.float32),
        ],
        compiler_params=params(),
        cost_estimate=pl.CostEstimate(flops=2 * 10**10, bytes_accessed=10**7, transcendentals=0),
        name="potential",
    )(gathered, *[jnp.asarray(table) for table in tables])


def all_charges(copies):
    bricks, pmes = lax.axis_size("brick"), lax.axis_size("pme")
    arrived = lax.all_to_all(copies, ("brick", "pme"), split_axis=0, concat_axis=0, tiled=True)
    return arrived.reshape(bricks, pmes, *copies.shape[1:])


def per_device(
    features,
    cotangent,
    neighbor_index,
    neighbor_count,
    edge_vector,
    quad_index,
    weight_basis,
    weight_radial,
    weight_scalar,
    weight_gate,
    weight_vector,
    weight_tensor,
    weight_charge,
    grid_base,
    grid_frac,
):
    atoms, width = features.shape
    channels = width // 4
    slots = neighbor_index.shape[0] // atoms
    ghost = quad_index.shape[3]
    table_rows = atoms + 12 * ghost
    hidden_units = weight_basis.shape[1]
    groups = halo_groups(lax.axis_size("brick"), lax.axis_size("pme"))
    message_shapes = [
        jax.ShapeDtypeStruct((len(cells) * ghost, width), jnp.bfloat16) for _, cells in groups
    ]

    outgoing = pl.pallas_call(
        functools.partial(pack_kernel, groups), out_shape=message_shapes, name="pack"
    )(quad_index, features)
    incoming = [shifted(value, *steps) for (steps, _), value in zip(groups, outgoing)]

    index_t = neighbor_index.reshape(atoms, slots).T
    vector_t = edge_vector.reshape(3, atoms, slots).transpose(0, 2, 1)
    hidden, unit, weight_t, features_t = pl.pallas_call(
        radial_kernel,
        out_shape=[
            jax.ShapeDtypeStruct((hidden_units, slots * atoms), jnp.bfloat16),
            jax.ShapeDtypeStruct((3, slots, atoms), jnp.float32),
            jax.ShapeDtypeStruct((7 * channels, hidden_units), jnp.bfloat16),
            jax.ShapeDtypeStruct((width, atoms), jnp.bfloat16),
        ],
        scratch_shapes=[pltpu.VMEM((weight_basis.shape[0], slots * atoms), jnp.float32)],
        compiler_params=params(),
        name="radial",
    )(vector_t, neighbor_count.reshape(1, atoms), weight_basis, weight_radial, features)

    block = SLOT_BLOCK * atoms
    steps = slots // (2 * SLOT_BLOCK)
    devices = lax.axis_size("brick") * lax.axis_size("pme")
    updated, charges, own_grad, *ghost_grads = pl.pallas_call(
        functools.partial(layer_kernel, groups),
        out_shape=[
            jax.ShapeDtypeStruct((atoms, 9 * channels), jnp.bfloat16),
            jax.ShapeDtypeStruct((devices, 8, atoms), jnp.float32),
            jax.ShapeDtypeStruct((atoms, width), jnp.float32),
        ]
        + message_shapes,
        scratch_shapes=[
            pltpu.VMEM((12 * ghost, width), jnp.bfloat16),
            pltpu.VMEM((width, table_rows), jnp.bfloat16),
            pltpu.VMEM((2 * steps, table_rows, block), jnp.bfloat16),
            pltpu.VMEM((steps + 1, 7 * channels, block), WORK),
            pltpu.VMEM((steps, 7 * channels, block), WORK),
            pltpu.VMEM((width, block), WORK),
            pltpu.VMEM((width, block), WORK),
            pltpu.VMEM((10, channels, atoms), jnp.float32),
            pltpu.VMEM((10, channels, atoms), jnp.float32),
            pltpu.VMEM((width, block), jnp.bfloat16),
            pltpu.VMEM((width, block), jnp.bfloat16),
            pltpu.VMEM((table_rows, width), jnp.float32),
        ],
        compiler_params=params(),
        name="layer",
    )(
        hidden,
        unit,
        index_t,
        weight_t,
        features_t,
        features,
        weight_scalar,
        weight_gate,
        weight_vector,
        weight_tensor,
        weight_charge.reshape(1, channels),
        cotangent,
        grid_base,
        grid_frac,
        *incoming,
    )
    gathered = all_charges(charges)
    potential = potential_block(gathered, GX, GY, NGZ)
    returned = [shifted(value, -steps[0], -steps[1]) for (steps, _), value in zip(groups, ghost_grads)]
    feature_grad = pl.pallas_call(
        functools.partial(gather_kernel, groups),
        in_specs=[pl.BlockSpec(memory_space=pltpu.VMEM)] * 2
        + [pl.BlockSpec(memory_space=pl.ANY)]
        + [pl.BlockSpec(memory_space=pltpu.VMEM)] * len(groups),
        out_shape=jax.ShapeDtypeStruct((atoms, width), jnp.float32),
        name="gather",
    )(quad_index, own_grad, potential, *returned)

    return (updated, feature_grad, potential)


def solution(mesh):
    placed = (
        P(("brick", "pme"), None),
        P(("brick", "pme"), None),
        P(("brick", "pme")),
        P(("brick", "pme")),
        P(None, ("brick", "pme")),
        P(("brick", "pme"), None, None, None),
        P(),
        P(),
        P(),
        P(),
        P(),
        P(),
        P(),
        P(None, ("brick", "pme")),
        P(None, ("brick", "pme")),
    )
    return jax.shard_map(
        per_device,
        mesh=mesh,
        in_specs=placed,
        out_specs=(P(("brick", "pme"), None), P(("brick", "pme"), None), P("brick", "pme", None)),
        check_vma=False,
    )
```

```python
import functools
import itertools
import math

import jax
import jax.numpy as jnp
import ml_dtypes
import numpy as np
from jax import lax
from jax.experimental import pallas as pl
from jax.experimental.pallas import tpu as pltpu
from jax.sharding import PartitionSpec as P

GX = 6
GY = 24
NGZ = 192

CUTOFF = 5.0
SMEAR = 1.0
COUPLING = 0.1
PRECISE = lax.Precision.HIGHEST
BORDER = ((0, 0), (0, 1), (0, 2), (0, 3), (1, 0), (1, 3), (2, 0), (2, 3), (3, 0), (3, 1), (3, 2), (3, 3))
SHIFT = (-1, 0, 0, 1)
QUARTER = (1, 0, 1, 0)
SLOT_BLOCK = 8
WORK = jnp.bfloat16
ROW_GROUP = 16
PIECE = 128
LINES = 16
SOLVE_UNROLL = 1
VMEM_LIMIT = 48 * 1024 * 1024


def halo_groups(brick_count, pme_count):
    groups = {}
    for cell, (row, col) in enumerate(BORDER):
        step = (SHIFT[row] % brick_count, SHIFT[col] % pme_count)
        groups.setdefault(step, []).append(cell)
    return tuple((step, tuple(cells)) for step, cells in groups.items())


def shifted(value, brick_step, pme_step):
    bricks, pmes = lax.axis_size("brick"), lax.axis_size("pme")
    pairs = []
    for b in range(bricks):
        for p in range(pmes):
            source = (b + brick_step) % bricks * pmes + (p + pme_step) % pmes
            pairs.append((source, b * pmes + p))
    return lax.ppermute(value, ("brick", "pme"), pairs)


def dot_t(left, right, dims, precision=None):
    return lax.dot_general(
        left, right, (dims, ((), ())), precision=precision, preferred_element_type=jnp.float32
    )


def dot_f32(left, right, dims=((1,), (0,))):
    return dot_t(left, right, dims, PRECISE)


def dot_node(left, right, dims=((1,), (0,))):
    left_high, left_low = split_f32(left)
    right_high, right_low = split_f32(right)
    return (
        dot_t(left_high, right_high, dims) + dot_t(left_high, right_low, dims) + dot_t(left_low, right_high, dims)
    )


def params(**kwargs):
    return pltpu.CompilerParams(vmem_limit_bytes=VMEM_LIMIT, **kwargs)


def quarter_onehot(quad_ref, atoms, quarters):
    index = jnp.concatenate([quad_ref[0, row, col : col + 1, :] for row, col in quarters], axis=1)
    rows = lax.broadcasted_iota(jnp.int32, (atoms, index.shape[1]), 0)
    return (rows == index).astype(jnp.bfloat16)


def pack_kernel(groups, quad_ref, features_ref, *message_refs):
    ghost = quad_ref.shape[3]
    chosen = quarter_onehot(quad_ref, features_ref.shape[0], ((0, 0), (0, 1), (1, 0), (1, 1)))
    picked = dot_t(chosen, features_ref[...], ((0,), (0,))).astype(jnp.bfloat16)
    for (_, cells), message_ref in zip(groups, message_refs):
        for place, cell in enumerate(cells):
            row, col = BORDER[cell]
            lower = (2 * QUARTER[row] + QUARTER[col]) * ghost
            message_ref[place * ghost : (place + 1) * ghost, :] = picked[lower : lower + ghost]


def radial_kernel(
    vector_ref,
    count_ref,
    basis_weight_ref,
    weight_radial_ref,
    features_ref,
    hidden_ref,
    unit_ref,
    weight_t_ref,
    features_t_ref,
    basis_ref,
):
    load_radial_weight(weight_radial_ref, weight_t_ref)
    transpose_into(features_t_ref, features_ref)
    slots, atoms = vector_ref.shape[1:]
    orders = basis_weight_ref.shape[0]
    parts = [vector_ref[axis] for axis in range(3)]
    distance = jnp.sqrt(parts[0] * parts[0] + parts[1] * parts[1] + parts[2] * parts[2])
    inverse = 1.0 / distance
    for axis in range(3):
        unit_ref[axis] = parts[axis] * inverse
    theta = distance * (math.pi / CUTOFF)
    cosine = jnp.cos(theta)
    live = lax.broadcasted_iota(jnp.int32, (slots, atoms), 0) < count_ref[...]
    envelope = jnp.where(live, 0.5 * (cosine + 1.0), 0.0)
    before = jnp.zeros_like(theta)
    current = jnp.sin(theta) * envelope
    for order in range(orders):
        for slot in range(slots):
            basis_ref[order : order + 1, slot * atoms : (slot + 1) * atoms] = current[slot : slot + 1, :]
        before, current = current, 2.0 * cosine * current - before
    width = 8 * atoms
    for start in range(0, slots * atoms, width):
        inner = dot_f32(basis_weight_ref[...], basis_ref[:, start : start + width], ((0,), (0,)))
        hidden_ref[:, start : start + width] = (inner * jax.nn.sigmoid(inner)).astype(jnp.bfloat16)


def load_radial_weight(weight_ref, weight_t_ref):
    channels = weight_ref.shape[1] // 7
    for path in range(7):
        block = weight_ref[:, path * channels : (path + 1) * channels].astype(jnp.float32)
        if path == 3:
            block = block - weight_ref[:, 4 * channels : 5 * channels].astype(jnp.float32) * (1.0 / 3.0)
        weight_t_ref[path * channels : (path + 1) * channels, :] = block.T.astype(jnp.bfloat16)


def transpose_into(out_ref, rows_ref):
    for lower in range(0, out_ref.shape[0], 128):
        out_ref[lower : lower + 128, :] = (
            rows_ref[:, lower : lower + 128].astype(jnp.float32).T.astype(jnp.bfloat16)
        )


def sender_onehot(index_ref, first, slots, table_rows):
    rows = lax.broadcasted_iota(jnp.int32, (table_rows, index_ref.shape[1]), 0)
    return jnp.concatenate(
        [(rows == index_ref[pl.ds(first + slot, 1), :]).astype(jnp.bfloat16) for slot in range(slots)], axis=1
    )


def unit_rows(unit_ref, first, slot):
    shape = (ROW_GROUP, unit_ref.shape[2])
    rows = [unit_ref[axis, pl.ds(first + slot, 1), :] for axis in range(3)]
    return [jnp.broadcast_to(row, shape).astype(WORK) for row in rows]


def tree_sum(terms):
    while len(terms) > 1:
        terms = [sum(terms[i + 1 : i + 2], terms[i]) for i in range(0, len(terms), 2)]
    return terms[0]


def radial_rows(radial_ref, weight_t_ref, hidden_ref, first, slots, atoms):
    for lower in range(0, slots, 2):
        lanes = pl.ds(pl.multiple_of((first + lower) * atoms, 2 * atoms), 2 * atoms)
        hidden = hidden_ref[:, lanes]
        for row in range(0, radial_ref.shape[0], PIECE):
            radial_ref[row : row + PIECE, lower * atoms : (lower + 2) * atoms] = dot_t(
                weight_t_ref[row : row + PIECE, :], hidden, ((1,), (0,))
            ).astype(WORK)
            yield


def interleave(vector_steps, matrix_steps):
    vector_steps, matrix_steps = iter(vector_steps), iter(matrix_steps)
    done = object()
    going = True
    while going:
        going = next(vector_steps, done) is not done
        for _ in range(3):
            going = (next(matrix_steps, done) is not done) or going


def layer_kernel(
    groups,
    hidden_ref,
    unit_ref,
    index_ref,
    weight_t_ref,
    features_t_ref,
    features_ref,
    weight_scalar_ref,
    weight_gate_ref,
    weight_vector_ref,
    weight_tensor_ref,
    weight_charge_ref,
    cotangent_ref,
    grid_base_ref,
    grid_frac_ref,
    *rest,
):
    count = len(groups)
    message_refs = rest[:count]
    updated_ref, charge_ref, own_grad_ref, *back_refs = rest[count : 2 * count + 3]
    (
        ghosts_ref,
        table_t_ref,
        chosen_ref,
        radial_even,
        radial_odd,
        sender_a,
        sender_b,
        total_ref,
        node_grad_ref,
        grad_a,
        grad_b,
        table_grad_ref,
    ) = rest[2 * count + 3 :]
    atoms, width = features_ref.shape
    channels = width // 4
    ghost = ghosts_ref.shape[0] // 12
    table_rows = table_t_ref.shape[1]
    slots = SLOT_BLOCK
    blocks = index_ref.shape[0] // slots
    steps = blocks // 2

    def products(block, radial_ref, sender_ref):
        first = block * slots
        yield from radial_rows(radial_ref, weight_t_ref, hidden_ref, first, slots, atoms)
        for lower in range(0, slots, 2):
            chosen = sender_onehot(index_ref, first + lower, 2, table_rows)
            chosen_ref[block, :, lower * atoms : (lower + 2) * atoms] = chosen
            for row in range(0, width, PIECE):
                sender_ref[row : row + PIECE, lower * atoms : (lower + 2) * atoms] = dot_t(
                    table_t_ref[row : row + PIECE, :], chosen, ((1,), (0,))
                ).astype(WORK)
                yield

    def messages(block, radial_ref, sender_ref):
        first = block * slots
        units = [unit_rows(unit_ref, first, slot) for slot in range(slots)]
        for row in range(0, channels, ROW_GROUP):
            terms = [[] for _ in range(10)]
            for slot in range(slots):
                lanes = slice(slot * atoms, (slot + 1) * atoms)
                unit = units[slot]
                paths = [
                    radial_ref[path * channels + row : path * channels + row + ROW_GROUP, lanes]
                    for path in range(7)
                ]
                scalar, *vector = [
                    sender_ref[part * channels + row : part * channels + row + ROW_GROUP, lanes]
                    for part in range(4)
                ]
                along = unit[0] * vector[0] + unit[1] * vector[1] + unit[2] * vector[2]
                terms[0].append(paths[0] * scalar + paths[1] * along)
                pushed = paths[2] * scalar + paths[4] * along
                twisted = paths[5] * scalar
                mixed = []
                for axis in range(3):
                    terms[1 + axis].append(unit[axis] * pushed + paths[3] * vector[axis])
                    mixed.append(unit[axis] * twisted + paths[6] * vector[axis])
                    terms[4 + axis].append(unit[axis] * mixed[axis])
                for place, (left, right) in enumerate(((0, 1), (1, 2), (0, 2))):
                    terms[7 + place].append(unit[left] * mixed[right] + unit[right] * mixed[left])
            for number in range(10):
                total_ref[number, row : row + ROW_GROUP, :] += tree_sum(terms[number]).astype(jnp.float32)
            yield

    for (_, cells), message_ref in zip(groups, message_refs):
        for place, cell in enumerate(cells):
            ghosts_ref[cell * ghost : (cell + 1) * ghost, :] = message_ref[
                place * ghost : (place + 1) * ghost, :
            ]
    table_t_ref[:, :atoms] = features_t_ref[...]
    transpose_into(table_t_ref.at[:, atoms:], ghosts_ref)
    total_ref[...] = jnp.zeros_like(total_ref)
    for _ in products(0, radial_even.at[0], sender_a):
        pass

    def forward_step(step, carry):
        interleave(
            messages(2 * step, radial_even.at[step], sender_a),
            products(2 * step + 1, radial_odd.at[step], sender_b),
        )
        following = jnp.minimum(2 * step + 2, blocks - 1)
        interleave(
            messages(2 * step + 1, radial_odd.at[step], sender_b),
            products(following, radial_even.at[step + 1], sender_a),
        )
        return carry

    lax.fori_loop(0, steps, forward_step, 0)
    scale = 1.0 / math.sqrt(index_ref.shape[0])
    trace = (total_ref[4] + total_ref[5] + total_ref[6]) * (1.0 / 3.0)
    sums = [total_ref[0], total_ref[1], total_ref[2], total_ref[3]]
    sums += [total_ref[4] - trace, total_ref[5] - trace]
    sums += [0.5 * total_ref[7], 0.5 * total_ref[8], 0.5 * total_ref[9]]
    aggregate = [(block * scale).T for block in sums]
    columns = lambda ref, block: ref[:, block * channels : (block + 1) * channels].astype(jnp.float32)
    gate = jax.nn.sigmoid(dot_node(aggregate[0], weight_gate_ref[...]))
    inner = dot_node(aggregate[0], weight_scalar_ref[...])
    inner_sigmoid = jax.nn.sigmoid(inner)
    vectors = dot_node(jnp.concatenate(aggregate[1:4], axis=0), weight_vector_ref[...])
    tensors = dot_node(jnp.concatenate(aggregate[4:9], axis=0), weight_tensor_ref[...])
    gate_v, gate_t = gate[:, :channels], gate[:, channels:]
    scalar_out = (columns(features_ref, 0) + inner * inner_sigmoid).astype(jnp.bfloat16)
    updated_ref[:, :channels] = scalar_out
    charge = dot_f32(weight_charge_ref[...], scalar_out.astype(jnp.float32), ((1,), (1,)))
    base, own_lines = grid_base_ref[...], lax.axis_index("pme") * GY
    rows = [charge, base[0:1], base[1:2] + own_lines, base[2:3], grid_frac_ref[...], jnp.zeros_like(charge)]
    rows = jnp.concatenate([row.astype(jnp.float32) for row in rows], axis=0)
    for device in range(charge_ref.shape[0]):
        charge_ref[device] = rows
    grad_v, grad_t = [], []
    gate_grad_v = jnp.zeros((atoms, channels), jnp.float32)
    gate_grad_t = jnp.zeros((atoms, channels), jnp.float32)
    for axis in range(3):
        value = vectors[axis * atoms : (axis + 1) * atoms]
        given = columns(cotangent_ref, 1 + axis)
        updated_ref[:, (1 + axis) * channels : (2 + axis) * channels] = (
            columns(features_ref, 1 + axis) + gate_v * value
        ).astype(jnp.bfloat16)
        gate_grad_v = gate_grad_v + given * value
        grad_v.append(given * gate_v)
    for block in range(5):
        value = tensors[block * atoms : (block + 1) * atoms]
        given = columns(cotangent_ref, 4 + block)
        updated_ref[:, (4 + block) * channels : (5 + block) * channels] = (gate_t * value).astype(
            jnp.bfloat16
        )
        gate_grad_t = gate_grad_t + given * value
        grad_t.append(given * gate_t)
    inner_grad = columns(cotangent_ref, 0) * (
        inner_sigmoid * (1.0 + inner * (1.0 - inner_sigmoid))
    )
    gate_grad = jnp.concatenate([gate_grad_v, gate_grad_t], axis=1) * (gate * (1.0 - gate))
    across = ((1,), (1,))
    grad_s = dot_node(inner_grad, weight_scalar_ref[...], across)
    grad_s = grad_s + dot_node(gate_grad, weight_gate_ref[...], across)
    grad_v = dot_node(jnp.concatenate(grad_v, axis=0), weight_vector_ref[...], across)
    grad_t = dot_node(jnp.concatenate(grad_t, axis=0), weight_tensor_ref[...], across)
    t00, t11, t01, t12, t02 = [grad_t[block * atoms : (block + 1) * atoms] for block in range(5)]
    third = (t00 + t11) * (1.0 / 3.0)
    pieces = [grad_s] + [grad_v[axis * atoms : (axis + 1) * atoms] for axis in range(3)]
    pieces += [t00 - third, t11 - third, -third, 0.5 * t01, 0.5 * t12, 0.5 * t02]
    for block in range(10):
        node_grad_ref[block] = (pieces[block] * scale).T


    table_grad_ref[...] = jnp.zeros_like(table_grad_ref)
    grad_b[...] = jnp.zeros_like(grad_b)

    def collect(block, grad_ref):
        for lower in range(0, width, 2 * channels):
            table_grad_ref[:, lower : lower + 2 * channels] += dot_t(
                chosen_ref[block], grad_ref[lower : lower + 2 * channels, :], ((1,), (1,))
            )
            yield

    def gradients(block, radial_ref, grad_ref):
        first = block * slots
        units = [unit_rows(unit_ref, first, slot) for slot in range(slots)]
        for row in range(0, channels, ROW_GROUP):
            node = [node_grad_ref[number, row : row + ROW_GROUP, :].astype(WORK) for number in range(10)]
            g_s, g_v, diag = node[0], node[1:4], node[4:7]
            off_01, off_12, off_02 = node[7:10]
            for slot in range(slots):
                lanes = slice(slot * atoms, (slot + 1) * atoms)
                unit = units[slot]
                paths = [
                    radial_ref[path * channels + row : path * channels + row + ROW_GROUP, lanes]
                    for path in range(7)
                ]
                along = unit[0] * g_v[0] + unit[1] * g_v[1] + unit[2] * g_v[2]
                bent = [
                    unit[0] * diag[0] + unit[1] * off_01 + unit[2] * off_02,
                    unit[0] * off_01 + unit[1] * diag[1] + unit[2] * off_12,
                    unit[0] * off_02 + unit[1] * off_12 + unit[2] * diag[2],
                ]
                twice = unit[0] * bent[0] + unit[1] * bent[1] + unit[2] * bent[2]
                pushed = paths[1] * g_s + paths[4] * along
                parts = [paths[0] * g_s + paths[2] * along + paths[5] * twice]
                for axis in range(3):
                    parts.append(unit[axis] * pushed + paths[3] * g_v[axis] + paths[6] * bent[axis])
                for number, part in enumerate(parts):
                    lower = number * channels + row
                    grad_ref[lower : lower + ROW_GROUP, lanes] = part.astype(jnp.bfloat16)
            yield

    def backward_step(step, carry):
        before = jnp.maximum(2 * step - 1, 0)
        interleave(gradients(2 * step, radial_even.at[step], grad_a), collect(before, grad_b))
        interleave(gradients(2 * step + 1, radial_odd.at[step], grad_b), collect(2 * step, grad_a))
        return carry

    lax.fori_loop(0, steps, backward_step, 0)
    for _ in collect(blocks - 1, grad_b):
        pass
    own_grad_ref[...] = table_grad_ref[:atoms, :] + cotangent_ref[:, :width].astype(jnp.float32)
    for (_, cells), back_ref in zip(groups, back_refs):
        for place, cell in enumerate(cells):
            lower = atoms + cell * ghost
            back_ref[place * ghost : (place + 1) * ghost, :] = table_grad_ref[
                lower : lower + ghost, :
            ].astype(jnp.bfloat16)


def gather_kernel(groups, quad_ref, own_ref, _, *rest):
    message_refs, out_ref = rest[: len(groups)], rest[len(groups)]
    order = [BORDER[cell] for _, cells in groups for cell in cells]
    quarters = [(QUARTER[row], QUARTER[col]) for row, col in order]
    chosen = quarter_onehot(quad_ref, own_ref.shape[0], quarters)
    messages = jnp.concatenate([message_ref[...] for message_ref in message_refs], axis=0)
    out_ref[...] = own_ref[...] + dot_t(chosen, messages, ((1,), (0,)))


def whole(shape):
    return pl.BlockSpec(shape, lambda step: (0,) * len(shape))


def split_f32(value):
    high = value.astype(jnp.bfloat16)
    return high, (value - high.astype(jnp.float32)).astype(jnp.bfloat16)


def split_np(value):
    high = value.astype(ml_dtypes.bfloat16)
    low = (value - high.astype(np.float64)).astype(ml_dtypes.bfloat16)
    return np.concatenate([high, low], axis=0)


def hartley_np(points):
    angle = 2.0 * np.pi / points * (np.outer(np.arange(points), np.arange(points)) % points)
    return np.cos(angle) + np.sin(angle)


def damping_np(points):
    index = np.arange(points)
    folded = np.minimum(index, points - index) / points
    modulus = 0.75 + 0.25 * np.cos(2.0 * np.pi / points * index)
    return folded**2, np.exp(-2.0 * np.pi**2 * SMEAR**2 * folded**2) / modulus**2


def grid_tables(bricks, cells_x, cells_y, full_y, cells_z):
    full_x = bricks * cells_x
    wave_x, wave_y, wave_z = hartley_np(full_x), hartley_np(full_y), hartley_np(cells_z)
    (square_x, damp_x), (_, damp_y), (square_z, damp_z) = map(damping_np, (full_x, full_y, cells_z))
    window = (np.arange(bricks)[:, None] * cells_x + np.arange(-1, cells_x + 1)[None, :]) % full_x
    own_x = np.zeros((bricks, cells_x + 2, full_x))
    own_x[:, :cells_x] = (wave_x * damp_x[None, :]).reshape(bricks, cells_x, full_x)
    own_x = np.concatenate([split_np(block) for block in own_x], axis=0)
    scale = COUPLING / (full_x * full_y * cells_z)
    extra = -cells_z % 128
    tail = lambda value, fill, axis: np.pad(
        value, [(0, extra) if dim == axis else (0, 0) for dim in range(value.ndim)], constant_values=fill
    )
    square_z = tail(square_z, 1.0, 0)
    return (
        split_np(tail(wave_z, 0.0, 0)),
        split_np(wave_y),
        split_np(wave_x[:, window.reshape(-1)]),
        own_x,
        (wave_y * damp_y[None, :]).astype(np.float32),
        tail(wave_z * damp_z[:, None] * scale, 0.0, 0).astype(np.float32),
        square_x.reshape(-1, 1).astype(np.float32),
        square_z.reshape(1, -1).astype(np.float32),
    )


def spline_rows(cells, base, offset, points):
    weights = (
        0.5 * (0.5 - offset) * (0.5 - offset),
        0.75 - offset * offset,
        0.5 * (0.5 + offset) * (0.5 + offset),
    )
    below, above = base - 1.0, base + 1.0
    if points:
        below = jnp.where(below < 0.0, below + points, below)
        above = jnp.where(above >= points, above - points, above)
    table = jnp.where(cells == above, weights[2], 0.0)
    table = jnp.where(cells == below, weights[0], table)
    return jnp.where(cells == base, weights[1], table)


def dot_split(left, right, dims=((1,), (0,))):
    rows = left.shape[0] // 2
    both = dot_t(left, right[0], dims)
    return both[:rows] + both[rows:] + dot_t(left[:rows], right[1], dims)


def cell_numbers(rows, lanes):
    return lax.broadcasted_iota(jnp.int32, (rows, lanes), 0).astype(jnp.float32)


def potential_kernel(
    cells_y,
    atoms_ref,
    wave_z_ref,
    wave_y_ref,
    wave_x_ref,
    own_x_ref,
    own_y_ref,
    own_z_ref,
    square_x_ref,
    square_z_ref,
    out_ref,
    shape_z_ref,
    lines_ref,
    square_ref,
    planes_ref,
):
    step = pl.program_id(0)
    bricks, pieces, _, piece_atoms = atoms_ref.shape
    atoms = pieces * piece_atoms
    cells_x, _, cells_z = out_ref.shape
    window = cells_x + 2
    full_y = planes_ref.shape[0]
    lanes_z = square_ref.shape[1]
    chunk = lines_ref.shape[1] // lanes_z

    @pl.when(step == 0)
    def _():
        square_ref[...] = square_x_ref[...] + square_z_ref[...]

        def tables(brick, carry):
            block = jnp.concatenate([atoms_ref[brick, piece] for piece in range(pieces)], axis=1)
            row = lambda number: block[number : number + 1, :]
            table = spline_rows(cell_numbers(cells_z, atoms), row(3), row(6), float(cells_z))
            high, low = split_f32(dot_split(wave_z_ref[...], split_f32(table)))
            shape_z_ref[brick, 0], shape_z_ref[brick, 1] = high, low
            return carry

        lax.fori_loop(0, bricks, tables, 0, unroll=8)

    first = step * chunk

    def spread(brick, carry):
        block = jnp.concatenate([atoms_ref[brick, piece] for piece in range(pieces)], axis=1)
        row = lambda number: block[number : number + 1, :]
        along_x = row(0) * spline_rows(cell_numbers(window, atoms) - 1.0, row(1), row(4), 0)
        table = spline_rows(cell_numbers(full_y, atoms), row(2), row(5), float(full_y))
        wave_y = jnp.concatenate(
            [wave_y_ref[pl.ds(pl.multiple_of(first + part, 16), chunk), :] for part in (0, full_y)], axis=0
        )
        along_y = dot_split(wave_y, split_f32(table))
        rows = jnp.concatenate([along_y[line : line + 1, :] * along_x for line in range(chunk)], axis=0)
        high, low = split_f32(rows)
        z_high, z_low = shape_z_ref[brick, 0], shape_z_ref[brick, 1]
        across = ((1,), (1,))
        grid = dot_t(high, z_high, across) + dot_t(high, z_low, across) + dot_t(low, z_high, across)
        place = pl.ds(pl.multiple_of(brick * window, window), window)
        for line in range(chunk):
            lines_ref[place, line * lanes_z : (line + 1) * lanes_z] = grid[line * window : (line + 1) * window]
        return carry

    lax.fori_loop(0, bricks, spread, 0, unroll=8)
    own = pl.multiple_of(lax.axis_index("brick") * (2 * window), 2 * window)

    def solve(batch, carry):
        lanes = pl.ds(pl.multiple_of(batch * (LINES * lanes_z), LINES * lanes_z), LINES * lanes_z)
        wave = dot_split(wave_x_ref[...], split_f32(lines_ref[:, lanes]))
        squares = []
        for line in range(LINES):
            number = first + batch * LINES + line
            height = jnp.minimum(number, full_y - number).astype(jnp.float32) * (1.0 / full_y)
            squares.append(square_ref[...] + height * height)
        square = jnp.concatenate(squares, axis=1)
        inverse = pl.reciprocal(square, approx=True)
        inverse = inverse * (2.0 - square * inverse)
        wave = wave * jnp.where(square > 0.0, inverse, 0.0)
        planes = dot_split(own_x_ref[pl.ds(own, 2 * window), :], split_f32(wave))
        for line in range(LINES):
            planes_ref[first + batch * LINES + line] = planes[:, line * lanes_z : (line + 1) * lanes_z]
        return carry

    lax.fori_loop(0, chunk // LINES, solve, 0, unroll=SOLVE_UNROLL)

    @pl.when(step == pl.num_programs(0) - 1)
    def _():
        along_y = own_y_ref[pl.ds(pl.multiple_of(lax.axis_index("pme") * cells_y, 8), cells_y), :]
        lines = [dot_f32(along_y, planes_ref[:, plane, :]) for plane in range(cells_x)]
        block = dot_f32(jnp.concatenate(lines, axis=0), own_z_ref[...])
        out_ref[...] = block.reshape(cells_x, cells_y, cells_z)


def potential_block(gathered, cells_x, cells_y, cells_z):
    bricks, pieces, rows, piece_atoms = gathered.shape
    full_y = cells_y * pieces
    atoms = pieces * piece_atoms
    window = cells_x + 2
    tables = grid_tables(bricks, cells_x, cells_y, full_y, cells_z)
    chunk = full_y if full_y <= 48 else 16
    lanes_z = cells_z + -cells_z % 128
    return pl.pallas_call(
        functools.partial(potential_kernel, cells_y),
        grid=(full_y // chunk,),
        in_specs=[whole(gathered.shape)] + [whole(table.shape) for table in tables],
        out_specs=whole((cells_x, cells_y, cells_z)),
        out_shape=jax.ShapeDtypeStruct((cells_x, cells_y, cells_z), jnp.float32),
        scratch_shapes=[
            pltpu.VMEM((bricks, 2, lanes_z, atoms), jnp.bfloat16),
            pltpu.VMEM((bricks * window, chunk * lanes_z), jnp.float32),
            pltpu.VMEM((bricks * cells_x, lanes_z), jnp.float32),
            pltpu.VMEM((full_y, window, lanes_z), jnp.float32),
        ],
        compiler_params=params(),
        cost_estimate=pl.CostEstimate(flops=2 * 10**10, bytes_accessed=10**7, transcendentals=0),
        name="potential",
    )(gathered, *[jnp.asarray(table) for table in tables])


def all_charges(copies):
    bricks, pmes = lax.axis_size("brick"), lax.axis_size("pme")
    arrived = lax.all_to_all(copies, ("brick", "pme"), split_axis=0, concat_axis=0, tiled=True)
    return arrived.reshape(bricks, pmes, *copies.shape[1:])


def per_device(
    features,
    cotangent,
    neighbor_index,
    neighbor_count,
    edge_vector,
    quad_index,
    weight_basis,
    weight_radial,
    weight_scalar,
    weight_gate,
    weight_vector,
    weight_tensor,
    weight_charge,
    grid_base,
    grid_frac,
):
    atoms, width = features.shape
    channels = width // 4
    slots = neighbor_index.shape[0] // atoms
    ghost = quad_index.shape[3]
    table_rows = atoms + 12 * ghost
    hidden_units = weight_basis.shape[1]
    groups = halo_groups(lax.axis_size("brick"), lax.axis_size("pme"))
    message_shapes = [
        jax.ShapeDtypeStruct((len(cells) * ghost, width), jnp.bfloat16) for _, cells in groups
    ]

    outgoing = pl.pallas_call(
        functools.partial(pack_kernel, groups), out_shape=message_shapes, name="pack"
    )(quad_index, features)
    incoming = [shifted(value, *steps) for (steps, _), value in zip(groups, outgoing)]

    index_t = neighbor_index.reshape(atoms, slots).T
    vector_t = edge_vector.reshape(3, atoms, slots).transpose(0, 2, 1)
    hidden, unit, weight_t, features_t = pl.pallas_call(
        radial_kernel,
        out_shape=[
            jax.ShapeDtypeStruct((hidden_units, slots * atoms), jnp.bfloat16),
            jax.ShapeDtypeStruct((3, slots, atoms), jnp.float32),
            jax.ShapeDtypeStruct((7 * channels, hidden_units), jnp.bfloat16),
            jax.ShapeDtypeStruct((width, atoms), jnp.bfloat16),
        ],
        scratch_shapes=[pltpu.VMEM((weight_basis.shape[0], slots * atoms), jnp.float32)],
        compiler_params=params(),
        name="radial",
    )(vector_t, neighbor_count.reshape(1, atoms), weight_basis, weight_radial, features)

    block = SLOT_BLOCK * atoms
    steps = slots // (2 * SLOT_BLOCK)
    devices = lax.axis_size("brick") * lax.axis_size("pme")
    updated, charges, own_grad, *ghost_grads = pl.pallas_call(
        functools.partial(layer_kernel, groups),
        out_shape=[
            jax.ShapeDtypeStruct((atoms, 9 * channels), jnp.bfloat16),
            jax.ShapeDtypeStruct((devices, 8, atoms), jnp.float32),
            jax.ShapeDtypeStruct((atoms, width), jnp.float32),
        ]
        + message_shapes,
        scratch_shapes=[
            pltpu.VMEM((12 * ghost, width), jnp.bfloat16),
            pltpu.VMEM((width, table_rows), jnp.bfloat16),
            pltpu.VMEM((2 * steps, table_rows, block), jnp.bfloat16),
            pltpu.VMEM((steps + 1, 7 * channels, block), WORK),
            pltpu.VMEM((steps, 7 * channels, block), WORK),
            pltpu.VMEM((width, block), WORK),
            pltpu.VMEM((width, block), WORK),
            pltpu.VMEM((10, channels, atoms), jnp.float32),
            pltpu.VMEM((10, channels, atoms), jnp.float32),
            pltpu.VMEM((width, block), jnp.bfloat16),
            pltpu.VMEM((width, block), jnp.bfloat16),
            pltpu.VMEM((table_rows, width), jnp.float32),
        ],
        compiler_params=params(),
        name="layer",
    )(
        hidden,
        unit,
        index_t,
        weight_t,
        features_t,
        features,
        weight_scalar,
        weight_gate,
        weight_vector,
        weight_tensor,
        weight_charge.reshape(1, channels),
        cotangent,
        grid_base,
        grid_frac,
        *incoming,
    )
    gathered = all_charges(charges)
    potential = potential_block(gathered, GX, GY, NGZ)
    returned = [shifted(value, -steps[0], -steps[1]) for (steps, _), value in zip(groups, ghost_grads)]
    feature_grad = pl.pallas_call(
        functools.partial(gather_kernel, groups),
        in_specs=[pl.BlockSpec(memory_space=pltpu.VMEM)] * 2
        + [pl.BlockSpec(memory_space=pl.ANY)]
        + [pl.BlockSpec(memory_space=pltpu.VMEM)] * len(groups),
        out_shape=jax.ShapeDtypeStruct((atoms, width), jnp.float32),
        name="gather",
    )(quad_index, own_grad, potential, *returned)

    return (updated, feature_grad, potential)


def solution(mesh):
    placed = (
        P(("brick", "pme"), None),
        P(("brick", "pme"), None),
        P(("brick", "pme")),
        P(("brick", "pme")),
        P(None, ("brick", "pme")),
        P(("brick", "pme"), None, None, None),
        P(),
        P(),
        P(),
        P(),
        P(),
        P(),
        P(),
        P(None, ("brick", "pme")),
        P(None, ("brick", "pme")),
    )
    return jax.shard_map(
        per_device,
        mesh=mesh,
        in_specs=placed,
        out_specs=(P(("brick", "pme"), None), P(("brick", "pme"), None), P("brick", "pme", None)),
        check_vma=False,
    )
```
